128 devices in a mesh: pair: 8 (over z, core), virt: 16 (over y, x).
Axes of the slice: x: 4, y: 4, z: 4, core: 2. Of those that a mesh axis runs over, the one named last changes fastest.
Arguments:
- amplitudes: bfloat16 [8, 8, 2048, 2048], P('pair', None, 'virt'), may hold values from -6 to 6
- factor: bfloat16 [8192, 1024], P('virt'), may hold values from -0.125 to 0.125
- home: int32 [128], replicated, may hold values from 0 to 127, as said below
- domains: int32 [8, 32], P('pair'), may hold values from 0 to 127, as said below
- coupling: bfloat16 [1024, 1024], P('virt'), may hold values from -6 to 6
- hole_weight: bfloat16 [8, 3, 1024], P('pair', None, 'virt'), may hold values from -3 to 3
- virt_energy: float32 [8192], replicated, may hold values from 0.1 to 1
- occ_i: float32 [8], replicated, may hold values from -0.6 to -0.1
- occ_j: float32 [8], P('pair'), may hold values from -0.6 to -0.1
Outputs:
- residual: float32 [8, 8, 2048, 2048], P('pair', None, 'virt')
The draws below stay inside these ranges and needn't reach their ends.
Inputs may be any that keep to these rules, and one draw needn't show every extreme that they name: `home`: a permutation of the virtual tiles; device k of virt stores the factor rows of slots k * 8 to (k + 1) * 8 - 1. `domains`: each row lists 32 distinct virtual tiles; at most 4 of a row's tiles are stored on any one device of virt, and in every row some device stores exactly 4 of them.
All inputs are finite; a program needn't handle non-finite values.
Results may differ from the reference program's by a relative error of at most 0.0033.
Values may be sent and summed in bfloat16 or wider, within the bound.
A program may use at most 128 MiB of HBM per device.

```python
import jax
import jax.numpy as jnp
from jax import lax

TILE = 64
NV = 8192
NP = 1024
DOM = 32
CAP = 4
NI = 8
VTILES = 128
VT_DEV = 8
NJ = 8
DV = 2048


def domain_tables(key):
    home = jax.random.permutation(jax.random.fold_in(key, 11), VTILES).astype(jnp.int32)

    def one_row(row_key):
        keys = jax.random.split(row_key, 4)
        owner_ranks = jax.random.permutation(keys[0], VTILES // VT_DEV).astype(jnp.int32)
        bases = jax.random.randint(keys[1], (VTILES // VT_DEV,), 0, VT_DEV).astype(jnp.int32)
        picks = jax.random.permutation(keys[2], (VTILES // VT_DEV - 1) * CAP)[:DOM - CAP].astype(jnp.int32)
        holder_pos = jnp.concatenate([jnp.zeros((CAP,), jnp.int32), 1 + picks // CAP])
        within = jnp.concatenate([jnp.arange(CAP, dtype=jnp.int32), picks % CAP])
        holder = owner_ranks[holder_pos]
        slots = holder * VT_DEV + (bases[holder] + within) % VT_DEV
        order = jax.random.permutation(keys[3], DOM)
        return home[slots][order]
    row_keys = jax.random.split(jax.random.fold_in(key, 23), NJ)
    return (home, jax.vmap(one_row)(row_keys).astype(jnp.int32))


def draw_home(key, part):
    return domain_tables(key)[0]


def draw_domains(key, part):
    return domain_tables(key)[1]


def steps_of(rng, shape, pieces, low, high):
    loudness = 1.0
    for dim, parts in pieces:
        steps = jax.random.uniform(jax.random.fold_in(jax.random.fold_in(rng, 6), dim), (parts,), jnp.float32, low / len(pieces), high / len(pieces))
        loudness = loudness * jnp.repeat(jnp.exp(steps), shape[dim] // parts).reshape((-1,) + (1,) * (len(shape) - 1 - dim))
    return loudness


def centred(key, dims, scale, limit, shards=(), held_as=jnp.bfloat16):
    level = steps_of(key, dims, shards, -0.22, 0.18) if shards else 1.0
    entries = jax.random.normal(key, dims, jnp.float32) * scale * level
    return jnp.minimum(jnp.maximum(entries, -limit), limit).astype(held_as)


def setup_inputs(seed: int = 0) -> dict:
    key_of = jax.random.split(jax.random.key(seed), 10)
    return {
        "amplitudes": centred(key_of[0], (NJ, NI, DV, DV), 1.0, 6.0, ((0, 8), (2, 16))),
        "factor": centred(key_of[1], (NV, NP), DV ** -0.5, 0.125, ((0, 16),)),
        "home": draw_home(jax.random.fold_in(key_of[9], 71), 0),
        "domains": draw_domains(jax.random.fold_in(key_of[9], 71), 0),
        "coupling": centred(key_of[4], (NP, NP), 1.0, 6.0, ((0, 16),)),
        "hole_weight": centred(key_of[5], (NJ, 3, NP), 0.5, 3.0, ((0, 8), (2, 16))),
        "virt_energy": jnp.clip(jax.random.uniform(key_of[6], (NV,), jnp.float32, 0.1, 1.0), 0.1, 1.0),
        "occ_i": jnp.clip(jax.random.uniform(key_of[7], (NI,), jnp.float32, -0.6, -0.1), -0.6, -0.1),
        "occ_j": jnp.clip(-0.6 + 0.5 * jax.random.uniform(key_of[8], (NJ,), jnp.float32) ** steps_of(key_of[8], (NJ,), ((0, 8),), -0.2, 0.2), -0.6, -0.1),
    }


def reference(amplitudes, factor, home, domains, coupling, hole_weight, virt_energy, occ_i, occ_j):
    tile_ids = jnp.arange(VTILES, dtype=jnp.int32)
    slot_of = jnp.zeros((VTILES,), jnp.int32).at[home].set(tile_ids)
    tiles = factor.reshape(VTILES, TILE, NP)
    spots = jnp.arange(DV, dtype=jnp.int32)

    def domain_rows(domain_entry_row):
        return tiles[slot_of[domain_entry_row]].reshape(DV, NP)

    def project(args):
        amps_j, domain_entry_row = args
        domain_coefficient = domain_rows(domain_entry_row)

        def single(amp):
            half = jnp.dot(amp, domain_coefficient, preferred_element_type=jnp.float32).astype(jnp.bfloat16)
            return jnp.dot(domain_coefficient.T, half, preferred_element_type=jnp.float32).astype(jnp.bfloat16)

        return lax.map(single, amps_j)

    projected = lax.map(project, (amplitudes, domains))
    empty_block = jnp.zeros_like(projected[:1])
    below_all = jnp.concatenate([empty_block, projected[:-1]], axis=0)
    above_all = jnp.concatenate([projected[1:], empty_block], axis=0)
    core = coupling.T.astype(jnp.float32)

    def finish(args):
        amps_j, domain_entry_row, own, below, above, weight, energy_j = args
        domain_coefficient = domain_rows(domain_entry_row)
        orbitals = domain_entry_row[spots // TILE] * TILE + spots % TILE
        energies = virt_energy[orbitals]
        weight = weight.astype(jnp.float32)
        hole = (weight[0][None, None, :] * below.astype(jnp.float32)
                + weight[1][None, None, :] * own.astype(jnp.float32)
                + weight[2][None, None, :] * above.astype(jnp.float32))
        dressed = (core[None] * own.astype(jnp.float32) + hole).astype(jnp.bfloat16)

        def single(second_arguments):
            amp, dress, energy_i = second_arguments
            back = jnp.dot(domain_coefficient, dress, preferred_element_type=jnp.float32).astype(jnp.bfloat16)
            ladder = jnp.dot(back, domain_coefficient.T, preferred_element_type=jnp.float32)
            shift = energies[:, None] + energies[None, :] - energy_i - energy_j
            return ladder + shift * amp.astype(jnp.float32)

        return lax.map(single, (amps_j, dressed, occ_i))

    return lax.map(finish, (amplitudes, domains, projected, below_all, above_all, hole_weight, occ_j))
```

```python
import jax
import jax.numpy as jnp
from jax import lax
from jax.experimental import pallas as pl
from jax.experimental.pallas import tpu as pltpu
from jax.sharding import PartitionSpec as P

TILE = 64
CAP = 4
SIDE = 4
PLANE = SIDE * SIDE
CHUNK = 2
MESH = pl.DeviceIdType.MESH
NT = (((1,), (1,)), ((), ()))
NN = (((1,), (0,)), ((), ()))
TN = (((0,), (0,)), ((), ()))


def dot(a, b, dims):
    return lax.dot_general(a, b, dims, preferred_element_type=jnp.float32)


def exchange_kernel(
    local_ref,
    place_ref,
    factor_ref,
    amp_hbm,
    coupling_ref,
    weight_ref,
    dt_out,
    back_out,
    amp,
    pack,
    got,
    dt,
    hbuf,
    recvh,
    proj,
    below,
    above,
    dressed,
    bbuf,
    io_sem,
    pack_sem,
    got_sem,
    ag_send,
    ag_recv,
    h_send,
    h_recv,
    p_send,
    below_sem,
    above_sem,
    b_send,
    b_recv,
):
    pairs = lax.axis_size("pair")
    pair = lax.axis_index("pair")
    me = lax.axis_index("virt")
    y, x = lax.div(me, SIDE), lax.rem(me, SIDE)
    after = lax.rem(pair + 1, pairs)
    before = lax.rem(pair + pairs - 1, pairs)
    blk = dt.shape[0] // PLANE
    rows = amp.shape[0] // hbuf.shape[0]
    chunks = hbuf.shape[0] // CHUNK

    barrier = pltpu.get_barrier_semaphore()

    @pl.loop(1, PLANE)
    def _(s):
        pl.semaphore_signal(
            barrier, inc=1, device_id=(pair, lax.rem(me + s, PLANE)), device_id_type=MESH
        )

    pl.semaphore_signal(barrier, inc=1, device_id=(after, me), device_id_type=MESH)
    pl.semaphore_signal(barrier, inc=1, device_id=(before, me), device_id_type=MESH)

    load = pltpu.make_async_copy(amp_hbm, amp, io_sem.at[0])
    load.start()

    for c in range(CAP // 2):
        two = jnp.concatenate(
            [factor_ref[local_ref[2 * c]], factor_ref[local_ref[2 * c + 1]]], axis=0
        )
        pack[c] = two.T

    pl.semaphore_wait(barrier, PLANE + 1)

    def pack_part(d):
        return pack.at[:, pl.ds(pl.multiple_of(d * blk, blk), blk), :]

    here = got.at[pl.ds(me * (CAP // 2), CAP // 2)]

    @pl.loop(1, PLANE)
    def _(s):
        d = lax.rem(me + s, PLANE)
        pltpu.make_async_remote_copy(
            pack_part(d), here, pack_sem, got_sem, device_id=(pair, d), device_id_type=MESH
        ).start()

    pltpu.make_async_copy(pack_part(me), here, got_sem).start()
    pltpu.make_async_copy(got, got, got_sem).wait()

    def pick(t):
        wide = got[place_ref[0, t]]
        return jnp.where(place_ref[1, t] == 1, wide[:, TILE:], wide[:, :TILE])

    own = pl.ds(pl.multiple_of(me * blk, blk), blk)
    for u in range(dt.shape[1] // (2 * TILE)):
        dt[own, u * 2 * TILE : (u + 1) * 2 * TILE] = jnp.concatenate(
            [pick(2 * u), pick(2 * u + 1)], axis=1
        )

    def at(axis, along, across):
        dx, dy = (along, across) if axis == 0 else (across, along)
        return lax.rem(y + dy + SIDE, SIDE) * SIDE + lax.rem(x + dx + SIDE, SIDE)

    hb, qb = blk // 2, blk // 4
    names = {}

    def message(kind, h, s, sign):
        k = names.setdefault((kind, h, s, sign), len(names))
        if kind == "a1":
            block, to = at(h, 0, 0), at(h, sign, 0)
        elif kind == "a2":
            block, to = at(h, -sign, 0), at(h, sign, 0)
        elif kind == "b1":
            block, to = at(h, s, 0), at(h, 0, sign)
        else:
            block, to = at(h, s, -sign), at(h, 0, sign)
        if kind in ("a1", "b1"):
            off, n = h * hb, hb
        else:
            off, n = h * hb + (0 if sign > 0 else qb), qb
        part = dt.at[pl.ds(pl.multiple_of(block * blk + off, qb), n), :]
        return pltpu.make_async_remote_copy(
            part, part, ag_send.at[k], ag_recv.at[k], device_id=(pair, to), device_id_type=MESH
        )

    def each(kind, offsets, do):
        for s in offsets:
            for h in (0, 1):
                for sign in (1, -1):
                    do(message(kind, h, s, sign))

    def go(m):
        m.start()

    def landed(m):
        m.wait_recv()

    each("a1", (0,), go)
    each("b1", (0,), go)
    for h in (0, 1):
        for sign in (1, -1):
            message("a1", h, 0, sign).wait_recv()
            message("a2", h, 0, sign).start()
    each("b1", (1, -1), go)
    each("b1", (0,), landed)
    each("b2", (0,), go)
    each("a2", (0,), landed)
    each("b1", (2,), go)
    each("b1", (1, -1), landed)
    each("b2", (1, -1), go)
    each("b1", (2,), landed)
    each("b2", (2,), go)
    each("b2", (0, 1, -1, 2), landed)

    store = pltpu.make_async_copy(dt, dt_out, io_sem.at[1])
    store.start()
    load.wait()

    def send(src, dst, send_sem, recv_sem, d):
        @pl.when(d != me)
        def _():
            pltpu.make_async_remote_copy(
                src, dst, send_sem, recv_sem, device_id=(pair, d), device_id_type=MESH
            ).start()

        @pl.when(d == me)
        def _():
            pltpu.make_async_copy(src, dst, recv_sem).start()

    @pl.loop(0, chunks)
    def _(c):
        now = pl.ds(c * CHUNK, CHUNK)

        @pl.loop(0, SIDE)
        def _(k):
            r = lax.rem(y + k, SIDE)
            band = pl.ds(pl.multiple_of(r * SIDE * blk, SIDE * blk), SIDE * blk)
            lines = pl.ds(pl.multiple_of(c * CHUNK * rows, CHUNK * rows), CHUNK * rows)
            part = dot(dt[band, :], amp[lines, :], NT).astype(jnp.bfloat16)
            for i in range(CHUNK):
                hbuf[c * CHUNK + i, band, :] = part[:, i * rows : (i + 1) * rows]
            for w in range(SIDE):
                d = r * SIDE + lax.rem(x + w, SIDE)
                send(
                    hbuf.at[now, pl.ds(pl.multiple_of(d * blk, blk), blk), :],
                    recvh.at[now, :, pl.ds(pl.multiple_of(me * rows, rows), rows)],
                    h_send,
                    h_recv.at[c],
                    d,
                )

    def project(c):
        now = pl.ds(c * CHUNK, CHUNK)
        pltpu.make_async_copy(recvh.at[now], recvh.at[now], h_recv.at[c]).wait()
        left = recvh[now].reshape(CHUNK * blk, recvh.shape[2])
        step = 256
        for n in range(dt.shape[0] // step):
            cols = slice(n * step, (n + 1) * step)
            part = dot(left, dt[cols, :], NT).astype(jnp.bfloat16)
            proj[now, :, cols] = part.reshape(CHUNK, blk, step)
        pltpu.make_async_remote_copy(
            proj.at[now], below.at[now], p_send.at[0], below_sem.at[c],
            device_id=(after, me), device_id_type=MESH,
        ).start()
        pltpu.make_async_remote_copy(
            proj.at[now], above.at[now], p_send.at[1], above_sem.at[c],
            device_id=(before, me), device_id_type=MESH,
        ).start()

    def finish(c):
        now = pl.ds(c * CHUNK, CHUNK)
        pltpu.make_async_copy(below.at[now], below.at[now], below_sem.at[c]).wait()
        pltpu.make_async_copy(above.at[now], above.at[now], above_sem.at[c]).wait()
        f32 = jnp.float32
        for i in range(CHUNK):
            mine = proj[c * CHUNK + i].astype(f32)
            hole = (
                weight_ref[0] * below[c * CHUNK + i].astype(f32)
                + weight_ref[1] * mine
                + weight_ref[2] * above[c * CHUNK + i].astype(f32)
            )
            dressed[i * blk : (i + 1) * blk, :] = (
                coupling_ref[...].astype(f32) * mine + hole
            ).astype(jnp.bfloat16)

        @pl.loop(0, PLANE // 2)
        def _(k):
            two = lax.rem(lax.div(me, 2) + k, PLANE // 2)
            cols = pl.ds(pl.multiple_of(two * 2 * rows, 2 * rows), 2 * rows)
            part = dot(dressed[...], dt[:, cols], NN).astype(jnp.bfloat16)
            bbuf[now, :, cols] = part.reshape(CHUNK, blk, 2 * rows)
            for w in range(2):
                d = two * 2 + w
                send(
                    bbuf.at[now, :, pl.ds(pl.multiple_of(d * rows, rows), rows)],
                    back_out.at[now, own, :],
                    b_send,
                    b_recv,
                    d,
                )

    @pl.loop(0, chunks + 1)
    def _(c):
        @pl.when(c < chunks)
        def _():
            project(c)

        @pl.when(c > 0)
        def _():
            finish(c - 1)

    pltpu.make_async_copy(back_out, back_out, b_recv).wait()
    store.wait()

    def sent(ref, sem):
        pltpu.make_async_copy(ref, ref, sem).wait()

    sent(pack.at[:, pl.ds(blk, (PLANE - 1) * blk), :], pack_sem)
    sent(hbuf.at[:, pl.ds(blk, (PLANE - 1) * blk), :], h_send)
    sent(proj, p_send.at[0])
    sent(proj, p_send.at[1])
    sent(bbuf.at[:, :, pl.ds(rows, (PLANE - 1) * rows)], b_send)
    for kind, offsets in (("a1", (0,)), ("a2", (0,)), ("b1", (0, 1, -1, 2)), ("b2", (0, 1, -1, 2))):
        each(kind, offsets, lambda m: m.wait_send())


def ladder_kernel(occ_i_ref, occ_j_ref, back_ref, dt_ref, amp_ref, col_ref, row_ref, out_ref):
    step = pl.program_id(0)
    n = back_ref.shape[0]
    rows = back_ref.shape[2]
    left = jnp.concatenate([back_ref[i].T for i in range(n)], axis=0)
    shift = row_ref[...] + col_ref[...]
    wide = 512
    for b in range(dt_ref.shape[1] // wide):
        cols = slice(b * wide, (b + 1) * wide)
        part = dot(left, dt_ref[:, cols], NN)
        for i in range(n):
            out_ref[i, :, cols] = part[i * rows : (i + 1) * rows] + (
                shift[:, cols] - occ_i_ref[step * n + i] - occ_j_ref[0]
            ) * amp_ref[i, :, cols].astype(jnp.float32)


def on_device(amplitudes, factor, home, domains, coupling, hole_weight, virt_energy, occ_i, occ_j):
    pairs = lax.axis_size("pair")
    pair = lax.axis_index("pair")
    me = lax.axis_index("virt")
    amps = amplitudes[0]
    ni, rows, width = amps.shape
    stored, rank = factor.shape
    tiles_here = stored // TILE
    blk = rank // PLANE
    domain = domains[0]
    tiles = home.shape[0]

    slot = jnp.sum(
        jnp.where(
            home[None, :] == domain[:, None], jnp.arange(tiles, dtype=jnp.int32)[None, :], 0
        ),
        axis=1,
    )
    holder = slot // tiles_here
    order = jnp.arange(domain.shape[0], dtype=jnp.int32)
    nth = jnp.sum(
        ((holder[None, :] == holder[:, None]) & (order[None, :] < order[:, None])).astype(jnp.int32),
        axis=1,
    )
    local = jnp.sum(
        jnp.where(
            (holder == me)[None, :] & (nth[None, :] == jnp.arange(CAP, dtype=jnp.int32)[:, None]),
            (slot % tiles_here)[None, :],
            0,
        ),
        axis=1,
    )
    place = jnp.stack([holder * (CAP // 2) + nth // 2, nth % 2])

    weight = hole_weight[0].astype(jnp.float32)
    weight = jnp.stack(
        [
            jnp.where(pair > 0, weight[0], 0.0),
            weight[1],
            jnp.where(pair < pairs - 1, weight[2], 0.0),
        ]
    )[:, :, None]

    by_tile = virt_energy.reshape(tiles, TILE)
    col = jnp.sum(
        jnp.where(
            domain[:, None, None] == jnp.arange(tiles, dtype=jnp.int32)[None, :, None],
            by_tile[None],
            0.0,
        ),
        axis=1,
    ).reshape(width)
    row = lax.dynamic_slice_in_dim(col, me * rows, rows)

    bf16 = jnp.bfloat16
    smem = pl.BlockSpec(memory_space=pltpu.SMEM)
    vmem = pl.BlockSpec(memory_space=pltpu.VMEM)
    anywhere = pl.BlockSpec(memory_space=pl.ANY)
    dma = pltpu.SemaphoreType.DMA
    chunks = ni // CHUNK
    dt, back = pl.pallas_call(
        exchange_kernel,
        out_shape=(
            jax.ShapeDtypeStruct((rank, width), bf16),
            jax.ShapeDtypeStruct((ni, rank, rows), bf16),
        ),
        in_specs=[smem, smem, vmem, anywhere, vmem, vmem],
        out_specs=(anywhere, anywhere),
        scratch_shapes=[
            pltpu.VMEM((ni * rows, width), bf16),
            pltpu.VMEM((CAP // 2, rank, 2 * TILE), bf16),
            pltpu.VMEM((PLANE * CAP // 2, blk, 2 * TILE), bf16),
            pltpu.VMEM((rank, width), bf16),
            pltpu.VMEM((ni, rank, rows), bf16),
            pltpu.VMEM((ni, blk, width), bf16),
            pltpu.VMEM((ni, blk, rank), bf16),
            pltpu.VMEM((ni, blk, rank), bf16),
            pltpu.VMEM((ni, blk, rank), bf16),
            pltpu.VMEM((CHUNK * blk, rank), bf16),
            pltpu.VMEM((ni, blk, width), bf16),
            dma((2,)),
            dma,
            dma,
            dma((40,)),
            dma((40,)),
            dma,
            dma((chunks,)),
            dma((2,)),
            dma((chunks,)),
            dma((chunks,)),
            dma,
            dma,
        ],
        compiler_params=pltpu.CompilerParams(
            collective_id=0, has_side_effects=True, vmem_limit_bytes=48 * 2**20
        ),
    )(
        local,
        place,
        factor.reshape(tiles_here, TILE, rank),
        amps.reshape(ni * rows, width),
        coupling,
        weight,
    )

    n = 2
    residual = pl.pallas_call(
        ladder_kernel,
        grid=(ni // n,),
        out_shape=jax.ShapeDtypeStruct((ni, rows, width), jnp.float32),
        in_specs=[
            smem,
            smem,
            pl.BlockSpec((n, rank, rows), lambda i: (i, 0, 0)),
            pl.BlockSpec((rank, width), lambda i: (0, 0)),
            pl.BlockSpec((n, rows, width), lambda i: (i, 0, 0)),
            pl.BlockSpec((1, width), lambda i: (0, 0)),
            pl.BlockSpec((rows, 1), lambda i: (0, 0)),
        ],
        out_specs=pl.BlockSpec((n, rows, width), lambda i: (i, 0, 0)),
        compiler_params=pltpu.CompilerParams(vmem_limit_bytes=32 * 2**20),
    )(occ_i, occ_j, back, dt, amps, col[None, :], row[:, None])
    return residual[None]


def solution(mesh):
    placed = (
        P("pair", None, "virt", None),
        P("virt", None),
        P(),
        P("pair", None),
        P("virt", None),
        P("pair", None, "virt"),
        P(),
        P(),
        P("pair"),
    )
    return jax.shard_map(
        on_device,
        mesh=mesh,
        in_specs=placed,
        out_specs=P("pair", None, "virt", None),
        check_vma=False,
    )
```

```python
import jax
import jax.numpy as jnp
from jax import lax
from jax.experimental import pallas as pl
from jax.experimental.pallas import tpu as pltpu
from jax.sharding import PartitionSpec as P

TILE = 64
CAP = 4
SIDE = 4
PLANE = SIDE * SIDE
CHUNK = 2
MESH = pl.DeviceIdType.MESH
NT = (((1,), (1,)), ((), ()))
NN = (((1,), (0,)), ((), ()))


def dot(a, b, dims):
    return lax.dot_general(a, b, dims, preferred_element_type=jnp.float32)


def residual_kernel(
    factor_hbm,
    home_hbm,
    domain_hbm,
    amp_hbm,
    coupling_hbm,
    weight_hbm,
    energy_hbm,
    occ_i_hbm,
    occ_j,
    out_ref,
    factor,
    home,
    domain,
    amp,
    coupling,
    weight,
    energy,
    occ_i,
    table,
    where,
    columns,
    col,
    row,
    pack,
    got,
    dt,
    hbuf,
    recvh,
    proj,
    below,
    above,
    dressed,
    bbuf,
    recvb,
    io_sem,
    pack_sem,
    got_sem,
    ag_send,
    ag_recv,
    h_send,
    h_recv,
    p_send,
    below_sem,
    above_sem,
    b_send,
    b_recv,
):
    f32, bf16, i32 = jnp.float32, jnp.bfloat16, jnp.int32
    pairs = lax.axis_size("pair")
    pair = lax.axis_index("pair")
    me = lax.axis_index("virt")
    y, x = lax.div(me, SIDE), lax.rem(me, SIDE)
    after = lax.rem(pair + 1, pairs)
    before = lax.rem(pair + pairs - 1, pairs)
    rank, width = dt.shape
    blk = rank // PLANE
    rows = width // PLANE
    chunks = hbuf.shape[0] // CHUNK
    tiles_here = factor.shape[0]
    in_domain = width // TILE

    barrier = pltpu.get_barrier_semaphore()

    @pl.loop(1, PLANE)
    def _(s):
        pl.semaphore_signal(
            barrier, inc=1, device_id=(pair, lax.rem(me + s, PLANE)), device_id_type=MESH
        )

    pl.semaphore_signal(barrier, inc=1, device_id=(after, me), device_id_type=MESH)
    pl.semaphore_signal(barrier, inc=1, device_id=(before, me), device_id_type=MESH)

    def fetch(k, src, dst):
        copy = pltpu.make_async_copy(src, dst, io_sem.at[k])
        copy.start()
        return copy

    get_home = fetch(0, home_hbm, home)
    get_domain = fetch(1, domain_hbm, domain)
    get_factor = fetch(2, factor_hbm, factor)
    get_small = [
        fetch(3, coupling_hbm, coupling),
        fetch(4, weight_hbm, weight),
        fetch(5, energy_hbm, energy),
        fetch(6, occ_i_hbm, occ_i),
    ]
    get_amp = fetch(7, amp_hbm, amp)

    get_home.wait()
    get_domain.wait()
    tiles = home.shape[1]
    home_row = jnp.broadcast_to(home[...], (in_domain, tiles))
    domain_row = jnp.broadcast_to(domain[...], (tiles, in_domain))
    slots = lax.broadcasted_iota(i32, (in_domain, tiles), 1)
    slot_col = jnp.max(jnp.where(home_row == domain_row.T, slots, 0), axis=1, keepdims=True)
    slots = lax.broadcasted_iota(i32, (tiles, in_domain), 0)
    slot_row = jnp.max(jnp.where(home_row.T == domain_row, slots, 0), axis=0, keepdims=True)
    holder_col, holder_row = lax.div(slot_col, tiles_here), lax.div(slot_row, tiles_here)
    same = holder_col == holder_row
    up = lax.broadcasted_iota(i32, (in_domain, in_domain), 0)
    across = lax.broadcasted_iota(i32, (in_domain, in_domain), 1)
    nth_row = jnp.sum(jnp.where(same & (up < across), 1, 0), axis=0, keepdims=True)
    nth_col = jnp.sum(jnp.where(same & (across < up), 1, 0), axis=1, keepdims=True)
    nth_row, nth_col = jnp.minimum(nth_row, CAP - 1), jnp.minimum(nth_col, CAP - 1)
    number = lax.broadcasted_iota(i32, (in_domain, 128), 1)
    mine = jnp.max(
        jnp.where(
            (holder_col == me) & (nth_col == number), lax.rem(slot_col, tiles_here), 0
        ),
        axis=0,
        keepdims=True,
    )
    table[0:1, 0:in_domain] = holder_row * (CAP // 2) + lax.div(nth_row, 2)
    table[1:2, 0:in_domain] = lax.rem(nth_row, 2)
    table[2:3, 0:in_domain] = lax.div(domain[...], 2)
    table[3:4, 0:in_domain] = lax.rem(domain[...], 2)
    table[4:5, :] = mine
    table[5:8, :] = jnp.zeros((3, 128), i32)
    scalars = fetch(0, table, where)
    scalars.wait()

    get_factor.wait()
    for c in range(CAP // 2):
        two = jnp.concatenate([factor[where[4, 2 * c]], factor[where[4, 2 * c + 1]]], axis=0)
        pack[c] = two.T

    pl.semaphore_wait(barrier, PLANE + 1)

    def pack_part(d):
        return pack.at[:, pl.ds(pl.multiple_of(d * blk, blk), blk), :]

    here = got.at[pl.ds(me * (CAP // 2), CAP // 2)]

    @pl.loop(1, PLANE)
    def _(s):
        d = lax.rem(me + s, PLANE)
        pltpu.make_async_remote_copy(
            pack_part(d), here, pack_sem, got_sem, device_id=(pair, d), device_id_type=MESH
        ).start()

    pltpu.make_async_copy(pack_part(me), here, got_sem).start()

    for copy in get_small:
        copy.wait()

    def halves(wide, second):
        return jnp.where(second == 1, wide[:, TILE:], wide[:, :TILE])

    def energy_of(t):
        return halves(energy[pl.ds(where[2, t], 1), :], where[3, t])

    for u in range(in_domain // 2):
        col[:, u * 2 * TILE : (u + 1) * 2 * TILE] = jnp.concatenate(
            [energy_of(2 * u), energy_of(2 * u + 1)], axis=1
        )
    here_energy = col[:, pl.ds(pl.multiple_of(me * rows, rows), rows)]
    row[...] = jnp.broadcast_to(here_energy, (rows, rows)).T - occ_j[0]
    has = (jnp.where(pair > 0, 1.0, 0.0), 1.0, jnp.where(pair < pairs - 1, 1.0, 0.0))
    for d in range(3):
        line = weight[d : d + 1, :].astype(f32) * has[d]
        columns[d] = jnp.broadcast_to(line, (128, blk)).T

    pltpu.make_async_copy(got, got, got_sem).wait()

    own = pl.ds(pl.multiple_of(me * blk, blk), blk)

    def tile_of(t):
        return halves(got[where[0, t]], where[1, t])

    for u in range(in_domain // 2):
        dt[own, u * 2 * TILE : (u + 1) * 2 * TILE] = jnp.concatenate(
            [tile_of(2 * u), tile_of(2 * u + 1)], axis=1
        )

    def device(dy, dx):
        return lax.rem(y + dy + SIDE, SIDE) * SIDE + lax.rem(x + dx + SIDE, SIDE)

    def at(axis, along, other):
        return device(other, along) if axis == 0 else device(along, other)

    hb, qb = blk // 2, blk // 4
    names = {}

    def message(kind, h, s, sign):
        k = names.setdefault((kind, h, s, sign), len(names))
        if kind == "a1":
            block, to = at(h, 0, 0), at(h, sign, 0)
        elif kind == "a2":
            block, to = at(h, -sign, 0), at(h, sign, 0)
        elif kind == "b1":
            block, to = at(h, s, 0), at(h, 0, sign)
        else:
            block, to = at(h, s, -sign), at(h, 0, sign)
        if kind in ("a1", "b1"):
            off, n = h * hb, hb
        else:
            off, n = h * hb + (0 if sign > 0 else qb), qb
        part = dt.at[pl.ds(pl.multiple_of(block * blk + off, qb), n), :]
        return pltpu.make_async_remote_copy(
            part, part, ag_send.at[k], ag_recv.at[k], device_id=(pair, to), device_id_type=MESH
        )

    def each(kind, offsets, do):
        for s in offsets:
            for h in (0, 1):
                for sign in (1, -1):
                    do(message(kind, h, s, sign))

    def go(m):
        m.start()

    def landed(m):
        m.wait_recv()

    def send(src, dst, send_sem, recv_sem, d):
        pltpu.make_async_remote_copy(
            src, dst, send_sem, recv_sem, device_id=(pair, d), device_id_type=MESH
        ).start()

    def band_of(d):
        return pl.ds(pl.multiple_of(d * blk, blk), blk)

    def half_parts(c, d):
        now = pl.ds(c * CHUNK, CHUNK)
        return (
            hbuf.at[now, band_of(d), :],
            recvh.at[now, :, pl.ds(pl.multiple_of(me * rows, rows), rows)],
        )

    def half(c, owners):
        left = jnp.concatenate([dt[band_of(d), :] for d in owners], axis=0)
        lines = pl.ds(pl.multiple_of(c * CHUNK * rows, CHUNK * rows), CHUNK * rows)
        part = dot(left, amp[lines, :], NT).astype(bf16)
        for k, d in enumerate(owners):
            for i in range(CHUNK):
                hbuf[c * CHUNK + i, band_of(d), :] = part[
                    k * blk : (k + 1) * blk, i * rows : (i + 1) * rows
                ]

    def half_send(c, owners):
        for d in owners:
            src, dst = half_parts(c, d)
            send(src, dst, h_send, h_recv.at[c], d)

    in_row = [device(0, k) for k in range(1, SIDE)]
    in_column = [device(k, 0) for k in range(1, SIDE)]

    each("a1", (0,), go)
    each("b1", (0,), go)
    for h in (0, 1):
        for sign in (1, -1):
            message("a1", h, 0, sign).wait_recv()
            message("a2", h, 0, sign).start()
    each("b1", (1, -1), go)
    each("b1", (0,), landed)
    each("b2", (0,), go)
    each("a2", (0,), landed)
    each("b1", (2,), go)
    each("b2", (0,), landed)
    get_amp.wait()

    @pl.loop(0, chunks)
    def _(c):
        half(c, [me, *in_row])
        half(c, in_column)

    each("b1", (1, -1), landed)
    each("b2", (1, -1), go)
    each("b1", (2,), landed)
    each("b2", (2,), go)

    @pl.loop(0, chunks)
    def _(c):
        src, dst = half_parts(c, me)
        pltpu.make_async_copy(src, dst, h_recv.at[c]).start()
        half_send(c, [d for two in zip(in_row, in_column) for d in two])

    each("b2", (1, -1, 2), landed)

    @pl.loop(0, chunks)
    def _(c):
        @pl.loop(1, SIDE)
        def _(k):
            owners = [device(k, w) for w in range(1, SIDE)]
            half(c, owners)
            half_send(c, owners)

    def project(c):
        now = pl.ds(c * CHUNK, CHUNK)
        pltpu.make_async_copy(recvh.at[now], recvh.at[now], h_recv.at[c]).wait()
        left = recvh[now].reshape(CHUNK * blk, width)
        step = 256
        for n in range(rank // step):
            cols = slice(n * step, (n + 1) * step)
            part = dot(left, dt[cols, :], NT).astype(bf16)
            proj[now, :, cols] = part.reshape(CHUNK, blk, step)
        pltpu.make_async_remote_copy(
            proj.at[now], below.at[now], p_send.at[0], below_sem.at[c],
            device_id=(after, me), device_id_type=MESH,
        ).start()
        pltpu.make_async_remote_copy(
            proj.at[now], above.at[now], p_send.at[1], above_sem.at[c],
            device_id=(before, me), device_id_type=MESH,
        ).start()

    def finish(c):
        now = pl.ds(c * CHUNK, CHUNK)
        pltpu.make_async_copy(below.at[now], below.at[now], below_sem.at[c]).wait()
        pltpu.make_async_copy(above.at[now], above.at[now], above_sem.at[c]).wait()
        for i in range(CHUNK):
            mid = proj[c * CHUNK + i].astype(f32)
            hole = (
                columns[0][:, :1] * below[c * CHUNK + i].astype(f32)
                + columns[1][:, :1] * mid
                + columns[2][:, :1] * above[c * CHUNK + i].astype(f32)
            )
            dressed[i * blk : (i + 1) * blk, :] = (
                coupling[...].astype(f32) * mid + hole
            ).astype(bf16)

        @pl.loop(0, PLANE // 2)
        def _(k):
            two = lax.rem(lax.div(me, 2) + k, PLANE // 2)
            cols = pl.ds(pl.multiple_of(two * 2 * rows, 2 * rows), 2 * rows)
            part = dot(dressed[...], dt[:, cols], NN).astype(bf16)
            bbuf[now, :, cols] = part.reshape(CHUNK, blk, 2 * rows)
            for w in range(2):
                d = two * 2 + w
                src = bbuf.at[now, :, pl.ds(pl.multiple_of(d * rows, rows), rows)]
                dst = recvb.at[now, own, :]

                @pl.when(d != me)
                def _():
                    send(src, dst, b_send, b_recv.at[c], d)

                @pl.when(d == me)
                def _():
                    pltpu.make_async_copy(src, dst, b_recv.at[c]).start()

    @pl.loop(0, chunks + 1)
    def _(c):
        @pl.when(c < chunks)
        def _():
            project(c)

        @pl.when(c > 0)
        def _():
            finish(c - 1)

    @pl.loop(0, chunks)
    def _(c):
        now = pl.ds(c * CHUNK, CHUNK)
        pltpu.make_async_copy(recvb.at[now], recvb.at[now], b_recv.at[c]).wait()
        left = jnp.concatenate([recvb[c * CHUNK + i].T for i in range(CHUNK)], axis=0)
        wide = 512
        for b in range(width // wide):
            cols = slice(b * wide, (b + 1) * wide)
            part = dot(left, dt[:, cols], NN)
            for i in range(CHUNK):
                lines = pl.ds(pl.multiple_of((c * CHUNK + i) * rows, rows), rows)
                shift = row[:, :1] + (col[:, cols] - occ_i[c * CHUNK + i])
                out_ref[c * CHUNK + i, :, cols] = part[
                    i * rows : (i + 1) * rows
                ] + shift * amp[lines, cols].astype(f32)

    def sent(ref, sem):
        pltpu.make_async_copy(ref, ref, sem).wait()

    sent(pack.at[:, pl.ds(blk, (PLANE - 1) * blk), :], pack_sem)
    sent(hbuf.at[:, pl.ds(blk, (PLANE - 1) * blk), :], h_send)
    sent(proj, p_send.at[0])
    sent(proj, p_send.at[1])
    sent(bbuf.at[:, :, pl.ds(rows, (PLANE - 1) * rows)], b_send)
    for kind, offsets in (("a1", (0,)), ("a2", (0,)), ("b1", (0, 1, -1, 2)), ("b2", (0, 1, -1, 2))):
        each(kind, offsets, lambda m: m.wait_send())


def on_device(amplitudes, factor, home, domains, coupling, hole_weight, virt_energy, occ_i, occ_j):
    ni, rows, width = amplitudes.shape[1:]
    stored, rank = factor.shape
    tiles_here = stored // TILE
    tiles = home.shape[0]
    blk = rank // PLANE
    lines = virt_energy.shape[0] // (2 * TILE)

    f32, bf16, i32 = jnp.float32, jnp.bfloat16, jnp.int32
    dma = pltpu.SemaphoreType.DMA
    chunks = ni // CHUNK
    residual = pl.pallas_call(
        residual_kernel,
        out_shape=pltpu.VMEM((ni, rows, width), f32),
        in_specs=[pl.BlockSpec(memory_space=pltpu.HBM)] * 8
        + [pl.BlockSpec(memory_space=pltpu.SMEM)],
        out_specs=pl.BlockSpec(memory_space=pltpu.VMEM),
        scratch_shapes=[
            pltpu.VMEM((tiles_here, TILE, rank), bf16),
            pltpu.VMEM((1, tiles), i32),
            pltpu.VMEM(domains.shape, i32),
            pltpu.VMEM((ni * rows, width), bf16),
            pltpu.VMEM((blk, rank), bf16),
            pltpu.VMEM((3, blk), bf16),
            pltpu.VMEM((lines, 2 * TILE), f32),
            pltpu.SMEM((ni,), f32),
            pltpu.VMEM((8, 128), i32),
            pltpu.SMEM((8, 128), i32),
            pltpu.VMEM((3, blk, 128), f32),
            pltpu.VMEM((1, width), f32),
            pltpu.VMEM((rows, rows), f32),
            pltpu.VMEM((CAP // 2, rank, 2 * TILE), bf16),
            pltpu.VMEM((PLANE * CAP // 2, blk, 2 * TILE), bf16),
            pltpu.VMEM((rank, width), bf16),
            pltpu.VMEM((ni, rank, rows), bf16),
            pltpu.VMEM((ni, blk, width), bf16),
            pltpu.VMEM((ni, blk, rank), bf16),
            pltpu.VMEM((ni, blk, rank), bf16),
            pltpu.VMEM((ni, blk, rank), bf16),
            pltpu.VMEM((CHUNK * blk, rank), bf16),
            pltpu.VMEM((ni, blk, width), bf16),
            pltpu.VMEM((ni, rank, rows), bf16),
            dma((8,)),
            dma,
            dma,
            dma((40,)),
            dma((40,)),
            dma,
            dma((chunks,)),
            dma((2,)),
            dma((chunks,)),
            dma((chunks,)),
            dma,
            dma((chunks,)),
        ],
        compiler_params=pltpu.CompilerParams(
            collective_id=0, has_side_effects=True, vmem_limit_bytes=48 * 2**20
        ),
    )(
        factor.reshape(tiles_here, TILE, rank),
        home[None, :],
        domains,
        amplitudes.reshape(ni * rows, width),
        coupling,
        hole_weight[0],
        virt_energy.reshape(lines, 2 * TILE),
        occ_i,
        occ_j,
    )
    return residual[None]


def solution(mesh):
    placed = (
        P("pair", None, "virt", None),
        P("virt", None),
        P(),
        P("pair", None),
        P("virt", None),
        P("pair", None, "virt"),
        P(),
        P(),
        P("pair"),
    )
    return jax.shard_map(
        on_device,
        mesh=mesh,
        in_specs=placed,
        out_specs=P("pair", None, "virt", None),
        check_vma=False,
    )
```

```python
import jax
import jax.numpy as jnp
from jax import lax
from jax.experimental import pallas as pl
from jax.experimental.pallas import tpu as pltpu
from jax.sharding import PartitionSpec as P

TILE = 64
CAP = 4
SIDE = 4
PLANE = SIDE * SIDE
CHUNK = 2
MESH = pl.DeviceIdType.MESH
NT = (((1,), (1,)), ((), ()))
NN = (((1,), (0,)), ((), ()))


def dot(a, b, dims):
    return lax.dot_general(a, b, dims, preferred_element_type=jnp.float32)


def ladder_steps(width):
    return [slice(b, b + 512) for b in range(0, width, 512)]


def ladder_left(recvb, c):
    return jnp.concatenate([recvb[c * CHUNK + i].T for i in range(CHUNK)], axis=0)


def ladder_part(left, c, cols, dt, amp, col, row, occ_i, out, slot):
    rows = left.shape[0] // CHUNK
    part = dot(left, dt[:, cols], NN)
    for i in range(CHUNK):
        lines = pl.ds(pl.multiple_of((c * CHUNK + i) * rows, rows), rows)
        shift = row[:, :1] + (col[:, cols] - occ_i[c * CHUNK + i])
        out[slot * CHUNK + i, :, cols] = part[i * rows : (i + 1) * rows] + shift * amp[
            lines, cols
        ].astype(jnp.float32)


def last_kernel(occ_i, ladder, amp, dt, recvb, col, row, out_hbm, last, sem, last_sem):
    done = ladder.shape[0]
    c = done // CHUNK
    copies = [pltpu.make_async_copy(ladder.at[i], out_hbm.at[i], sem.at[i]) for i in range(done)]
    for copy in copies:
        copy.start()
    left = ladder_left(recvb, c)
    for k, cols in enumerate(ladder_steps(dt.shape[1])):
        ladder_part(left, c, cols, dt, amp, col, row, occ_i, last, 0)
        copy = pltpu.make_async_copy(
            last.at[:, :, cols], out_hbm.at[pl.ds(done, CHUNK), :, cols], last_sem.at[k]
        )
        copy.start()
        copies.append(copy)
    for copy in copies:
        copy.wait()


def residual_kernel(
    factor_hbm,
    home_hbm,
    domain_hbm,
    amp_hbm,
    coupling_hbm,
    weight_hbm,
    energy_hbm,
    occ_i_hbm,
    occ_j,
    ladder,
    amp,
    dt,
    recvb,
    col,
    row,
    factor,
    home,
    domain,
    coupling,
    weight,
    energy,
    occ_i,
    table,
    where,
    columns,
    pack,
    got_up,
    got_low,
    hbuf,
    recvh,
    proj,
    below,
    above,
    dressed,
    bbuf,
    io_sem,
    pack_sem,
    got_sem,
    ag_send,
    ag_recv,
    h_send,
    h_recv,
    p_send,
    below_sem,
    above_sem,
    b_send,
    b_recv,
):
    f32, bf16, i32 = jnp.float32, jnp.bfloat16, jnp.int32
    pairs = lax.axis_size("pair")
    pair = lax.axis_index("pair")
    me = lax.axis_index("virt")
    y, x = lax.div(me, SIDE), lax.rem(me, SIDE)
    after = lax.rem(pair + 1, pairs)
    before = lax.rem(pair + pairs - 1, pairs)
    rank, width = dt.shape
    blk = rank // PLANE
    rows = width // PLANE
    chunks = hbuf.shape[0] // CHUNK
    tiles_here = factor.shape[0]
    in_domain = width // TILE

    barrier = pltpu.get_barrier_semaphore()

    @pl.loop(1, PLANE)
    def _(s):
        pl.semaphore_signal(
            barrier, inc=1, device_id=(pair, lax.rem(me + s, PLANE)), device_id_type=MESH
        )

    pl.semaphore_signal(barrier, inc=1, device_id=(after, me), device_id_type=MESH)
    pl.semaphore_signal(barrier, inc=1, device_id=(before, me), device_id_type=MESH)

    def fetch(k, src, dst):
        copy = pltpu.make_async_copy(src, dst, io_sem.at[k])
        copy.start()
        return copy

    get_home = fetch(0, home_hbm, home)
    get_domain = fetch(1, domain_hbm, domain)
    get_factor = fetch(2, factor_hbm, factor)
    get_small = [
        fetch(3, coupling_hbm, coupling),
        fetch(4, weight_hbm, weight),
        fetch(5, energy_hbm, energy),
        fetch(6, occ_i_hbm, occ_i),
    ]
    get_amp = fetch(7, amp_hbm, amp)

    get_home.wait()
    get_domain.wait()
    tiles = home.shape[1]
    home_row = jnp.broadcast_to(home[...], (in_domain, tiles))
    domain_row = jnp.broadcast_to(domain[...], (tiles, in_domain))
    slots = lax.broadcasted_iota(i32, (in_domain, tiles), 1)
    slot_col = jnp.max(jnp.where(home_row == domain_row.T, slots, 0), axis=1, keepdims=True)
    slots = lax.broadcasted_iota(i32, (tiles, in_domain), 0)
    slot_row = jnp.max(jnp.where(home_row.T == domain_row, slots, 0), axis=0, keepdims=True)
    holder_col, holder_row = lax.div(slot_col, tiles_here), lax.div(slot_row, tiles_here)
    same = holder_col == holder_row
    up = lax.broadcasted_iota(i32, (in_domain, in_domain), 0)
    across = lax.broadcasted_iota(i32, (in_domain, in_domain), 1)
    nth_row = jnp.sum(jnp.where(same & (up < across), 1, 0), axis=0, keepdims=True)
    nth_col = jnp.sum(jnp.where(same & (across < up), 1, 0), axis=1, keepdims=True)
    nth_row, nth_col = jnp.minimum(nth_row, CAP - 1), jnp.minimum(nth_col, CAP - 1)
    number = lax.broadcasted_iota(i32, (in_domain, 128), 1)
    mine = jnp.max(
        jnp.where(
            (holder_col == me) & (nth_col == number), lax.rem(slot_col, tiles_here), 0
        ),
        axis=0,
        keepdims=True,
    )
    table[0:1, 0:in_domain] = holder_row * (CAP // 2) + lax.div(nth_row, 2)
    table[1:2, 0:in_domain] = lax.rem(nth_row, 2)
    table[2:3, 0:in_domain] = lax.div(domain[...], 2)
    table[3:4, 0:in_domain] = lax.rem(domain[...], 2)
    table[4:5, :] = mine
    table[5:8, :] = jnp.zeros((3, 128), i32)
    scalars = fetch(0, table, where)
    scalars.wait()

    get_factor.wait()
    for c in range(CAP // 2):
        two = jnp.concatenate([factor[where[4, 2 * c]], factor[where[4, 2 * c + 1]]], axis=0)
        pack[c] = two.T

    pl.semaphore_wait(barrier, PLANE + 1)

    hb, qb = blk // 2, blk // 4
    got = (got_up, got_low)

    def pack_part(d, h):
        return pack.at[:, pl.ds(pl.multiple_of(d * blk + h * hb, hb), hb), :]

    for h in range(2):
        here = got[h].at[pl.ds(me * (CAP // 2), CAP // 2)]

        @pl.loop(1, PLANE)
        def _(s):
            d = lax.rem(me + s, PLANE)
            pltpu.make_async_remote_copy(
                pack_part(d, h), here, pack_sem, got_sem.at[h],
                device_id=(pair, d), device_id_type=MESH,
            ).start()

        pltpu.make_async_copy(pack_part(me, h), here, got_sem.at[h]).start()

    for copy in get_small:
        copy.wait()

    def halves(wide, second):
        return jnp.where(second == 1, wide[:, TILE:], wide[:, :TILE])

    def energy_of(t):
        return halves(energy[pl.ds(where[2, t], 1), :], where[3, t])

    for u in range(in_domain // 2):
        col[:, u * 2 * TILE : (u + 1) * 2 * TILE] = jnp.concatenate(
            [energy_of(2 * u), energy_of(2 * u + 1)], axis=1
        )
    here_energy = col[:, pl.ds(pl.multiple_of(me * rows, rows), rows)]
    row[...] = jnp.broadcast_to(here_energy, (rows, rows)).T - occ_j[0]
    has = (jnp.where(pair > 0, 1.0, 0.0), 1.0, jnp.where(pair < pairs - 1, 1.0, 0.0))
    for d in range(3):
        line = weight[d : d + 1, :].astype(f32) * has[d]
        columns[d] = jnp.broadcast_to(line, (128, blk)).T

    own = pl.ds(pl.multiple_of(me * blk, blk), blk)

    def arrange(h):
        pltpu.make_async_copy(got[h], got[h], got_sem.at[h]).wait()
        lines = pl.ds(pl.multiple_of(me * blk + h * hb, hb), hb)
        for u in range(in_domain // 2):
            dt[lines, u * 2 * TILE : (u + 1) * 2 * TILE] = jnp.concatenate(
                [halves(got[h][where[0, t]], where[1, t]) for t in (2 * u, 2 * u + 1)], axis=1
            )

    def device(dy, dx):
        return lax.rem(y + dy + SIDE, SIDE) * SIDE + lax.rem(x + dx + SIDE, SIDE)

    def at(axis, along, other):
        return device(other, along) if axis == 0 else device(along, other)

    names = {}

    def message(kind, h, s, sign):
        k = names.setdefault((kind, h, s, sign), len(names))
        if kind == "a1":
            block, to = at(h, 0, 0), at(h, sign, 0)
        elif kind == "a2":
            block, to = at(h, -sign, 0), at(h, sign, 0)
        elif kind == "b1":
            block, to = at(h, s, 0), at(h, 0, sign)
        else:
            block, to = at(h, s, -sign), at(h, 0, sign)
        if kind in ("a1", "b1"):
            off, n = h * hb, hb
        else:
            off, n = h * hb + (0 if sign > 0 else qb), qb
        part = dt.at[pl.ds(pl.multiple_of(block * blk + off, qb), n), :]
        return pltpu.make_async_remote_copy(
            part, part, ag_send.at[k], ag_recv.at[k], device_id=(pair, to), device_id_type=MESH
        )

    def each(kind, offsets, do):
        for s in offsets:
            for h in (0, 1):
                for sign in (1, -1):
                    do(message(kind, h, s, sign))

    def go(m):
        m.start()

    def landed(m):
        m.wait_recv()

    def send(src, dst, send_sem, recv_sem, d):
        @pl.when(d != me)
        def _():
            pltpu.make_async_remote_copy(
                src, dst, send_sem, recv_sem, device_id=(pair, d), device_id_type=MESH
            ).start()

        @pl.when(d == me)
        def _():
            pltpu.make_async_copy(src, dst, recv_sem).start()

    def band_of(d):
        return pl.ds(pl.multiple_of(d * blk, blk), blk)

    def half(c, r):
        now = pl.ds(c * CHUNK, CHUNK)
        band = pl.ds(pl.multiple_of(r * SIDE * blk, SIDE * blk), SIDE * blk)
        lines = pl.ds(pl.multiple_of(c * CHUNK * rows, CHUNK * rows), CHUNK * rows)
        part = dot(dt[band, :], amp[lines, :], NT).astype(bf16)
        for i in range(CHUNK):
            hbuf[c * CHUNK + i, band, :] = part[:, i * rows : (i + 1) * rows]
        for w in range(SIDE):
            d = r * SIDE + lax.rem(x + w, SIDE)
            send(
                hbuf.at[now, band_of(d), :],
                recvh.at[now, :, pl.ds(pl.multiple_of(me * rows, rows), rows)],
                h_send,
                h_recv.at[c],
                d,
            )

    for h in (0, 1):
        arrange(h)
        for kind in ("a1", "b1"):
            for sign in (1, -1):
                message(kind, h, 0, sign).start()
    for h in (0, 1):
        for sign in (1, -1):
            message("a1", h, 0, sign).wait_recv()
            message("a2", h, 0, sign).start()
    each("b1", (1, -1), go)
    each("b1", (0,), landed)
    each("b2", (0,), go)
    each("a2", (0,), landed)
    each("b1", (2,), go)
    each("b2", (0,), landed)
    each("b1", (1, -1), landed)
    each("b2", (1, -1), go)
    each("b1", (2,), landed)
    each("b2", (2,), go)

    each("b2", (1, -1, 2), landed)
    get_amp.wait()

    @pl.loop(0, chunks)
    def _(c):
        @pl.loop(0, SIDE)
        def _(k):
            half(c, lax.rem(y + k, SIDE))

    def project(c):
        now = pl.ds(c * CHUNK, CHUNK)
        pltpu.make_async_copy(recvh.at[now], recvh.at[now], h_recv.at[c]).wait()
        left = recvh[now].reshape(CHUNK * blk, width)
        step = 256
        for n in range(rank // step):
            cols = slice(n * step, (n + 1) * step)
            part = dot(left, dt[cols, :], NT).astype(bf16)
            proj[now, :, cols] = part.reshape(CHUNK, blk, step)
        pltpu.make_async_remote_copy(
            proj.at[now], below.at[now], p_send.at[0], below_sem.at[c],
            device_id=(after, me), device_id_type=MESH,
        ).start()
        pltpu.make_async_remote_copy(
            proj.at[now], above.at[now], p_send.at[1], above_sem.at[c],
            device_id=(before, me), device_id_type=MESH,
        ).start()

    def finish(c):
        now = pl.ds(c * CHUNK, CHUNK)
        pltpu.make_async_copy(below.at[now], below.at[now], below_sem.at[c]).wait()
        pltpu.make_async_copy(above.at[now], above.at[now], above_sem.at[c]).wait()
        for i in range(CHUNK):
            mid = proj[c * CHUNK + i].astype(f32)
            hole = (
                columns[0][:, :1] * below[c * CHUNK + i].astype(f32)
                + columns[1][:, :1] * mid
                + columns[2][:, :1] * above[c * CHUNK + i].astype(f32)
            )
            dressed[i * blk : (i + 1) * blk, :] = (
                coupling[...].astype(f32) * mid + hole
            ).astype(bf16)

        @pl.loop(0, SIDE)
        def _(k):
            r = lax.rem(y + k, SIDE)
            cols = pl.ds(pl.multiple_of(r * SIDE * rows, SIDE * rows), SIDE * rows)
            part = dot(dressed[...], dt[:, cols], NN).astype(bf16)
            bbuf[now, :, cols] = part.reshape(CHUNK, blk, SIDE * rows)
            for w in range(SIDE):
                d = r * SIDE + lax.rem(x + w, SIDE)
                src = bbuf.at[now, :, pl.ds(pl.multiple_of(d * rows, rows), rows)]
                send(src, recvb.at[now, own, :], b_send, b_recv.at[c], d)

    @pl.loop(0, chunks + 1)
    def _(c):
        @pl.when(c < chunks)
        def _():
            project(c)

        @pl.when(c > 0)
        def _():
            finish(c - 1)

    @pl.loop(0, chunks)
    def _(c):
        now = pl.ds(c * CHUNK, CHUNK)
        pltpu.make_async_copy(recvb.at[now], recvb.at[now], b_recv.at[c]).wait()

        @pl.when(c < chunks - 1)
        def _():
            left = ladder_left(recvb, c)
            for cols in ladder_steps(width):
                ladder_part(left, c, cols, dt, amp, col, row, occ_i, ladder, c)

    def sent(ref, sem):
        pltpu.make_async_copy(ref, ref, sem).wait()

    sent(pack.at[:, pl.ds(blk, (PLANE - 1) * blk), :], pack_sem)
    sent(hbuf.at[:, pl.ds(blk, (PLANE - 1) * blk), :], h_send)
    sent(proj, p_send.at[0])
    sent(proj, p_send.at[1])
    sent(bbuf.at[:, :, pl.ds(rows, (PLANE - 1) * rows)], b_send)
    for kind, offsets in (("a1", (0,)), ("a2", (0,)), ("b1", (0, 1, -1, 2)), ("b2", (0, 1, -1, 2))):
        each(kind, offsets, lambda m: m.wait_send())


def on_device(amplitudes, factor, home, domains, coupling, hole_weight, virt_energy, occ_i, occ_j):
    ni, rows, width = amplitudes.shape[1:]
    stored, rank = factor.shape
    tiles_here = stored // TILE
    tiles = home.shape[0]
    blk = rank // PLANE
    lines = virt_energy.shape[0] // (2 * TILE)

    f32, bf16, i32 = jnp.float32, jnp.bfloat16, jnp.int32
    dma = pltpu.SemaphoreType.DMA
    chunks = ni // CHUNK
    done = ni - CHUNK
    vmem = pl.BlockSpec(memory_space=pltpu.VMEM)
    smem = pl.BlockSpec(memory_space=pltpu.SMEM)
    hbm = pl.BlockSpec(memory_space=pltpu.HBM)
    held = pl.pallas_call(
        residual_kernel,
        out_shape=(
            pltpu.VMEM((done, rows, width), f32),
            pltpu.VMEM((ni * rows, width), bf16),
            pltpu.VMEM((rank, width), bf16),
            pltpu.VMEM((ni, rank, rows), bf16),
            pltpu.VMEM((1, width), f32),
            pltpu.VMEM((rows, rows), f32),
        ),
        in_specs=[hbm] * 8 + [smem],
        out_specs=(vmem,) * 6,
        scratch_shapes=[
            pltpu.VMEM((tiles_here, TILE, rank), bf16),
            pltpu.VMEM((1, tiles), i32),
            pltpu.VMEM(domains.shape, i32),
            pltpu.VMEM((blk, rank), bf16),
            pltpu.VMEM((3, blk), bf16),
            pltpu.VMEM((lines, 2 * TILE), f32),
            pltpu.SMEM((ni,), f32),
            pltpu.VMEM((8, 128), i32),
            pltpu.SMEM((8, 128), i32),
            pltpu.VMEM((3, blk, 128), f32),
            pltpu.VMEM((CAP // 2, rank, 2 * TILE), bf16),
            pltpu.VMEM((PLANE * CAP // 2, blk // 2, 2 * TILE), bf16),
            pltpu.VMEM((PLANE * CAP // 2, blk // 2, 2 * TILE), bf16),
            pltpu.VMEM((ni, rank, rows), bf16),
            pltpu.VMEM((ni, blk, width), bf16),
            pltpu.VMEM((ni, blk, rank), bf16),
            pltpu.VMEM((ni, blk, rank), bf16),
            pltpu.VMEM((ni, blk, rank), bf16),
            pltpu.VMEM((CHUNK * blk, rank), bf16),
            pltpu.VMEM((ni, blk, width), bf16),
            dma((8,)),
            dma,
            dma((2,)),
            dma((40,)),
            dma((40,)),
            dma,
            dma((chunks,)),
            dma((2,)),
            dma((chunks,)),
            dma((chunks,)),
            dma,
            dma((chunks,)),
        ],
        compiler_params=pltpu.CompilerParams(
            collective_id=0, has_side_effects=True, vmem_limit_bytes=40 * 2**20
        ),
    )(
        factor.reshape(tiles_here, TILE, rank),
        home[None, :],
        domains,
        amplitudes.reshape(ni * rows, width),
        coupling,
        hole_weight[0],
        virt_energy.reshape(lines, 2 * TILE),
        occ_i,
        occ_j,
    )
    residual = pl.pallas_call(
        last_kernel,
        out_shape=jax.ShapeDtypeStruct((ni, rows, width), f32),
        in_specs=[smem] + [vmem] * 6,
        out_specs=hbm,
        scratch_shapes=[
            pltpu.VMEM((CHUNK, rows, width), f32),
            dma((done,)),
            dma((len(ladder_steps(width)),)),
        ],
        compiler_params=pltpu.CompilerParams(vmem_limit_bytes=16 * 2**20),
    )(occ_i, *held)
    return residual[None]


def solution(mesh):
    placed = (
        P("pair", None, "virt", None),
        P("virt", None),
        P(),
        P("pair", None),
        P("virt", None),
        P("pair", None, "virt"),
        P(),
        P(),
        P("pair"),
    )
    return jax.shard_map(
        on_device,
        mesh=mesh,
        in_specs=placed,
        out_specs=P("pair", None, "virt", None),
        check_vma=False,
    )
```

```python
import jax
import jax.numpy as jnp
from jax import lax
from jax.experimental import pallas as pl
from jax.experimental.pallas import tpu as pltpu
from jax.sharding import PartitionSpec as P

TILE = 64
CAP = 4
SIDE = 4
PLANE = SIDE * SIDE
CHUNK = 2
SHARE = 16
MESH = pl.DeviceIdType.MESH
NT = (((1,), (1,)), ((), ()))
NN = (((1,), (0,)), ((), ()))


def dot(a, b, dims):
    return lax.dot_general(a, b, dims, preferred_element_type=jnp.float32)


def ladder_steps(width):
    return [slice(b, b + 512) for b in range(0, width, 512)]


def ladder_left(recvb, c):
    return jnp.concatenate([recvb[c * CHUNK + i].T for i in range(CHUNK)], axis=0)


def ladder_part(left, c, cols, dt, amp, col, row, occ_i, out, slot):
    rows = left.shape[0] // CHUNK
    part = dot(left, dt[:, cols], NN)
    for i in range(CHUNK):
        lines = pl.ds(pl.multiple_of((c * CHUNK + i) * rows, rows), rows)
        shift = row[:, :1] + (col[:, cols] - occ_i[c * CHUNK + i])
        out[slot * CHUNK + i, :, cols] = part[i * rows : (i + 1) * rows] + shift * amp[
            lines, cols
        ].astype(jnp.float32)


def last_kernel(occ_i, ladder, amp, dt, recvb, col, row, out_hbm, last, sem, last_sem):
    done = ladder.shape[0]
    c = done // CHUNK
    copies = [pltpu.make_async_copy(ladder.at[i], out_hbm.at[i], sem.at[i]) for i in range(done)]
    for copy in copies:
        copy.start()
    left = ladder_left(recvb, c)
    for k, cols in enumerate(ladder_steps(dt.shape[1])):
        ladder_part(left, c, cols, dt, amp, col, row, occ_i, last, 0)
        copy = pltpu.make_async_copy(
            last.at[:, :, cols], out_hbm.at[pl.ds(done, CHUNK), :, cols], last_sem.at[k]
        )
        copy.start()
        copies.append(copy)
    for copy in copies:
        copy.wait()


def residual_kernel(
    factor_hbm,
    home_hbm,
    domain_hbm,
    amp_hbm,
    coupling_hbm,
    weight_hbm,
    energy_hbm,
    occ_i_hbm,
    occ_j,
    ladder,
    amp,
    dt,
    recvb,
    col,
    row,
    factor,
    home,
    domain,
    coupling,
    weight,
    energy,
    occ_i,
    table,
    where,
    columns,
    all_slots,
    slot_lists,
    full,
    ready,
    pack,
    got_up,
    got_low,
    hbuf,
    recvh,
    proj,
    below,
    above,
    dressed,
    bbuf,
    io_sem,
    slot_send,
    slot_recv,
    full_send,
    full_recv,
    share_out,
    share_in,
    pack_sem,
    got_sem,
    ag_send,
    ag_recv,
    h_send,
    h_recv,
    p_send,
    below_sem,
    above_sem,
    b_send,
    b_recv,
):
    f32, bf16, i32 = jnp.float32, jnp.bfloat16, jnp.int32
    pairs = lax.axis_size("pair")
    pair = lax.axis_index("pair")
    me = lax.axis_index("virt")
    y, x = lax.div(me, SIDE), lax.rem(me, SIDE)
    after = lax.rem(pair + 1, pairs)
    before = lax.rem(pair + pairs - 1, pairs)
    rank, width = dt.shape
    blk = rank // PLANE
    rows = width // PLANE
    chunks = hbuf.shape[0] // CHUNK
    tiles_here = factor.shape[0]
    in_domain = width // TILE

    barrier = pltpu.get_barrier_semaphore()

    @pl.loop(1, PLANE)
    def _(s):
        pl.semaphore_signal(
            barrier, inc=1, device_id=(pair, lax.rem(me + s, PLANE)), device_id_type=MESH
        )

    @pl.loop(1, pairs)
    def _(s):
        pl.semaphore_signal(
            barrier, inc=1, device_id=(lax.rem(pair + s, pairs), me), device_id_type=MESH
        )

    def fetch(k, src, dst):
        copy = pltpu.make_async_copy(src, dst, io_sem.at[k])
        copy.start()
        return copy

    get_home = fetch(0, home_hbm, home)
    get_domain = fetch(1, domain_hbm, domain)
    get_factor = fetch(2, factor_hbm, factor)
    get_small = [
        fetch(3, coupling_hbm, coupling),
        fetch(4, weight_hbm, weight),
        fetch(5, energy_hbm, energy),
        fetch(6, occ_i_hbm, occ_i),
    ]
    get_amp = fetch(7, amp_hbm, amp)

    get_home.wait()
    get_domain.wait()
    tiles = home.shape[1]
    home_row = jnp.broadcast_to(home[...], (in_domain, tiles))
    domain_row = jnp.broadcast_to(domain[...], (tiles, in_domain))
    slots = lax.broadcasted_iota(i32, (in_domain, tiles), 1)
    slot_col = jnp.max(jnp.where(home_row == domain_row.T, slots, 0), axis=1, keepdims=True)
    slots = lax.broadcasted_iota(i32, (tiles, in_domain), 0)
    slot_row = jnp.max(jnp.where(home_row.T == domain_row, slots, 0), axis=0, keepdims=True)
    holder_col, holder_row = lax.div(slot_col, tiles_here), lax.div(slot_row, tiles_here)
    same = holder_col == holder_row
    up = lax.broadcasted_iota(i32, (in_domain, in_domain), 0)
    across = lax.broadcasted_iota(i32, (in_domain, in_domain), 1)
    nth_row = jnp.sum(jnp.where(same & (up < across), 1, 0), axis=0, keepdims=True)
    nth_col = jnp.sum(jnp.where(same & (across < up), 1, 0), axis=1, keepdims=True)
    nth_row, nth_col = jnp.minimum(nth_row, CAP - 1), jnp.minimum(nth_col, CAP - 1)
    number = lax.broadcasted_iota(i32, (in_domain, 128), 1)
    mine = jnp.max(
        jnp.where(
            (holder_col == me) & (nth_col == number), lax.rem(slot_col, tiles_here), 0
        ),
        axis=0,
        keepdims=True,
    )
    table[0:1, 0:in_domain] = holder_row * (CAP // 2) + lax.div(nth_row, 2)
    table[1:2, 0:in_domain] = lax.rem(nth_row, 2)
    table[2:3, 0:in_domain] = lax.div(domain[...], 2)
    table[3:4, 0:in_domain] = lax.rem(domain[...], 2)
    table[4:5, :] = mine
    table[5:8, :] = jnp.zeros((3, 128), i32)
    scalars = fetch(0, table, where)
    all_slots[pair] = jnp.zeros((1, 128), i32)
    all_slots[pair, :, 0:in_domain] = slot_row
    scalars.wait()

    get_factor.wait()
    for c in range(CAP // 2):
        two = jnp.concatenate([factor[where[4, 2 * c]], factor[where[4, 2 * c + 1]]], axis=0)
        pack[c] = two.T

    keep = blk - SHARE
    per = PLANE // pairs
    rank_cols = pl.ds(pl.multiple_of(pair * per * blk, per * blk), per * blk)
    wide = factor[:, :, rank_cols].reshape(tiles_here * TILE, per * blk).T
    wide = jnp.concatenate([wide[k * blk + keep : (k + 1) * blk] for k in range(per)], axis=0)
    two_here = tiles_here // 2
    for k in range(two_here):
        full[me * two_here + k] = wide[:, k * 2 * TILE : (k + 1) * 2 * TILE]

    pl.semaphore_wait(barrier, PLANE + pairs - 2)

    hs = per * SHARE // 2

    @pl.loop(1, pairs)
    def _(s):
        pltpu.make_async_remote_copy(
            all_slots.at[pair], all_slots.at[pair], slot_send, slot_recv,
            device_id=(lax.rem(pair + s, pairs), me), device_id_type=MESH,
        ).start()

    def share_send(first, n, h, sem, to):
        part = full.at[pl.ds(first, n), h * hs : (h + 1) * hs, :]
        pltpu.make_async_remote_copy(
            part, part, full_send, full_recv.at[sem], device_id=(pair, to), device_id_type=MESH
        ).start()

    def to_x(s):
        return y * SIDE + lax.rem(x + s, SIDE)

    def to_y(s):
        return lax.rem(y + s, SIDE) * SIDE + x

    for s in range(1, SIDE):
        share_send(me * two_here, two_here, 0, 0, to_x(s))
        share_send(me * two_here, two_here, 1, 1, to_y(s))

    got = (got_up, got_low)
    offs = (0, got_up.shape[1])

    def pack_part(d, h):
        return pack.at[:, pl.ds(pl.multiple_of(d * blk + offs[h], 16), got[h].shape[1]), :]

    for h in range(2):
        here = got[h].at[pl.ds(me * (CAP // 2), CAP // 2)]

        @pl.loop(1, PLANE)
        def _(s):
            d = lax.rem(me + s, PLANE)
            pltpu.make_async_remote_copy(
                pack_part(d, h), here, pack_sem, got_sem.at[h],
                device_id=(pair, d), device_id_type=MESH,
            ).start()

        pltpu.make_async_copy(pack_part(me, h), here, got_sem.at[h]).start()

    for copy in get_small:
        copy.wait()

    def halves(wide, second):
        return jnp.where(second == 1, wide[:, TILE:], wide[:, :TILE])

    def energy_of(t):
        return halves(energy[pl.ds(where[2, t], 1), :], where[3, t])

    for u in range(in_domain // 2):
        col[:, u * 2 * TILE : (u + 1) * 2 * TILE] = jnp.concatenate(
            [energy_of(2 * u), energy_of(2 * u + 1)], axis=1
        )
    here_energy = col[:, pl.ds(pl.multiple_of(me * rows, rows), rows)]
    row[...] = jnp.broadcast_to(here_energy, (rows, rows)).T - occ_j[0]
    has = (jnp.where(pair > 0, 1.0, 0.0), 1.0, jnp.where(pair < pairs - 1, 1.0, 0.0))
    for d in range(3):
        line = weight[d : d + 1, :].astype(f32) * has[d]
        columns[d] = jnp.broadcast_to(line, (128, blk)).T

    def share_landed(n, h, sem):
        part = full.at[pl.ds(0, n), h * hs : (h + 1) * hs, :]
        pltpu.make_async_copy(part, part, full_recv.at[sem]).wait()

    share_landed((SIDE - 1) * two_here, 0, 0)
    for s in range(1, SIDE):
        share_send(y * SIDE * two_here, SIDE * two_here, 0, 2, to_y(s))
    share_landed((SIDE - 1) * two_here, 1, 1)
    for s in range(1, SIDE):
        for k in range(SIDE):
            share_send((k * SIDE + x) * two_here, two_here, 1, 3, to_x(s))

    own = pl.ds(pl.multiple_of(me * blk, blk), blk)

    def arrange(h):
        pltpu.make_async_copy(got[h], got[h], got_sem.at[h]).wait()
        lines = pl.ds(pl.multiple_of(me * blk + offs[h], 16), got[h].shape[1])
        for u in range(in_domain // 2):
            dt[lines, u * 2 * TILE : (u + 1) * 2 * TILE] = jnp.concatenate(
                [halves(got[h][where[0, t]], where[1, t]) for t in (2 * u, 2 * u + 1)], axis=1
            )

    def device(dy, dx):
        return lax.rem(y + dy + SIDE, SIDE) * SIDE + lax.rem(x + dx + SIDE, SIDE)

    def at(axis, along, other):
        return device(other, along) if axis == 0 else device(along, other)

    names = {}

    def message(kind, h, s, sign):
        k = names.setdefault((kind, h, s, sign), len(names))
        if kind == "a1":
            block, to = at(h, 0, 0), at(h, sign, 0)
        elif kind == "a2":
            block, to = at(h, -sign, 0), at(h, sign, 0)
        elif kind == "b1":
            block, to = at(h, s, 0), at(h, 0, sign)
        else:
            block, to = at(h, s, -sign), at(h, 0, sign)
        if kind in ("a1", "b1"):
            off, n = h * (width // 2), width // 2
        else:
            off, n = h * (width // 2) + (0 if sign > 0 else width // 4), width // 4
        part = dt.at[pl.ds(pl.multiple_of(block * blk, blk), keep), off : off + n]
        return pltpu.make_async_remote_copy(
            part, part, ag_send.at[k], ag_recv.at[k], device_id=(pair, to), device_id_type=MESH
        )

    def each(kind, offsets, do):
        for s in offsets:
            for h in (0, 1):
                for sign in (1, -1):
                    do(message(kind, h, s, sign))

    def go(m):
        m.start()

    def landed(m):
        m.wait_recv()

    def send(src, dst, send_sem, recv_sem, d):
        @pl.when(d != me)
        def _():
            pltpu.make_async_remote_copy(
                src, dst, send_sem, recv_sem, device_id=(pair, d), device_id_type=MESH
            ).start()

        @pl.when(d == me)
        def _():
            pltpu.make_async_copy(src, dst, recv_sem).start()

    def band_of(d):
        return pl.ds(pl.multiple_of(d * blk, blk), blk)

    def half(c, r):
        now = pl.ds(c * CHUNK, CHUNK)
        band = pl.ds(pl.multiple_of(r * SIDE * blk, SIDE * blk), SIDE * blk)
        lines = pl.ds(pl.multiple_of(c * CHUNK * rows, CHUNK * rows), CHUNK * rows)
        part = dot(dt[band, :], amp[lines, :], NT).astype(bf16)
        for i in range(CHUNK):
            hbuf[c * CHUNK + i, band, :] = part[:, i * rows : (i + 1) * rows]
        for w in range(SIDE):
            d = r * SIDE + lax.rem(x + w, SIDE)
            send(
                hbuf.at[now, band_of(d), :],
                recvh.at[now, :, pl.ds(pl.multiple_of(me * rows, rows), rows)],
                h_send,
                h_recv.at[c],
                d,
            )

    arrange(0)
    arrange(1)
    each("a1", (0,), go)
    each("b1", (0,), go)

    pltpu.make_async_copy(
        all_slots.at[pl.ds(0, pairs - 1)], all_slots.at[pl.ds(0, pairs - 1)], slot_recv
    ).wait()
    lists = fetch(0, all_slots, slot_lists)
    share_landed((SIDE - 1) * SIDE * two_here, 0, 2)
    share_landed((SIDE - 1) * SIDE * two_here, 1, 3)
    lists.wait()

    @pl.loop(0, pairs)
    def _(k):
        p = lax.rem(pair + pairs // 2 + k, pairs)
        for u in range(in_domain // 2):
            both = [slot_lists[p, 0, t] for t in (2 * u, 2 * u + 1)]
            ready[p, :, u * 2 * TILE : (u + 1) * 2 * TILE] = jnp.concatenate(
                [halves(full[lax.div(s, 2)], lax.rem(s, 2)) for s in both], axis=1
            )
        for b in range(per):
            src = ready.at[p, b * SHARE : (b + 1) * SHARE, :]
            start = pl.multiple_of((pair * per + b) * blk + keep, SHARE)
            dst = dt.at[pl.ds(start, SHARE), :]

            @pl.when(p != pair)
            def _():
                pltpu.make_async_remote_copy(
                    src, dst, share_out, share_in, device_id=(p, me), device_id_type=MESH
                ).start()

            @pl.when(p == pair)
            def _():
                pltpu.make_async_copy(src, dst, share_in).start()

    for h in (0, 1):
        for sign in (1, -1):
            message("a1", h, 0, sign).wait_recv()
            message("a2", h, 0, sign).start()
    each("b1", (1, -1), go)
    each("b1", (0,), landed)
    each("b2", (0,), go)
    each("a2", (0,), landed)
    each("b1", (2,), go)
    each("b2", (0,), landed)
    each("b1", (1, -1), landed)
    each("b2", (1, -1), go)
    each("b1", (2,), landed)
    each("b2", (2,), go)

    each("b2", (1, -1, 2), landed)
    all_shares = dt.at[pl.ds(0, PLANE * SHARE), :]
    pltpu.make_async_copy(all_shares, all_shares, share_in).wait()
    get_amp.wait()

    @pl.loop(0, chunks)
    def _(c):
        @pl.loop(0, SIDE)
        def _(k):
            half(c, lax.rem(y + k, SIDE))

    def project(c):
        now = pl.ds(c * CHUNK, CHUNK)
        pltpu.make_async_copy(recvh.at[now], recvh.at[now], h_recv.at[c]).wait()
        left = recvh[now].reshape(CHUNK * blk, width)
        step = 256
        for n in range(rank // step):
            cols = slice(n * step, (n + 1) * step)
            part = dot(left, dt[cols, :], NT).astype(bf16)
            proj[now, :, cols] = part.reshape(CHUNK, blk, step)
        pltpu.make_async_remote_copy(
            proj.at[now], below.at[now], p_send.at[0], below_sem.at[c],
            device_id=(after, me), device_id_type=MESH,
        ).start()
        pltpu.make_async_remote_copy(
            proj.at[now], above.at[now], p_send.at[1], above_sem.at[c],
            device_id=(before, me), device_id_type=MESH,
        ).start()

    def finish(c):
        now = pl.ds(c * CHUNK, CHUNK)
        pltpu.make_async_copy(below.at[now], below.at[now], below_sem.at[c]).wait()
        pltpu.make_async_copy(above.at[now], above.at[now], above_sem.at[c]).wait()
        for i in range(CHUNK):
            mid = proj[c * CHUNK + i].astype(f32)
            hole = (
                columns[0][:, :1] * below[c * CHUNK + i].astype(f32)
                + columns[1][:, :1] * mid
                + columns[2][:, :1] * above[c * CHUNK + i].astype(f32)
            )
            dressed[i * blk : (i + 1) * blk, :] = (
                coupling[...].astype(f32) * mid + hole
            ).astype(bf16)

        @pl.loop(0, SIDE)
        def _(k):
            r = lax.rem(y + k, SIDE)
            cols = pl.ds(pl.multiple_of(r * SIDE * rows, SIDE * rows), SIDE * rows)
            part = dot(dressed[...], dt[:, cols], NN).astype(bf16)
            bbuf[now, :, cols] = part.reshape(CHUNK, blk, SIDE * rows)
            for w in range(SIDE):
                d = r * SIDE + lax.rem(x + w, SIDE)
                src = bbuf.at[now, :, pl.ds(pl.multiple_of(d * rows, rows), rows)]
                send(src, recvb.at[now, own, :], b_send, b_recv.at[c], d)

    @pl.loop(0, chunks + 1)
    def _(c):
        @pl.when(c < chunks)
        def _():
            project(c)

        @pl.when(c > 0)
        def _():
            finish(c - 1)

    @pl.loop(0, chunks)
    def _(c):
        now = pl.ds(c * CHUNK, CHUNK)
        pltpu.make_async_copy(recvb.at[now], recvb.at[now], b_recv.at[c]).wait()

        @pl.when(c < chunks - 1)
        def _():
            left = ladder_left(recvb, c)
            for cols in ladder_steps(width):
                ladder_part(left, c, cols, dt, amp, col, row, occ_i, ladder, c)

    def sent(ref, sem):
        pltpu.make_async_copy(ref, ref, sem).wait()

    sent(pack.at[:, pl.ds(0, (PLANE - 1) * keep), :], pack_sem)
    sent(all_slots.at[pl.ds(0, pairs - 1)], slot_send)
    units = (SIDE - 1) * (2 + 2 * SIDE) * two_here
    sent(full.at[pl.ds(0, units // 2)], full_send)
    sent(ready.at[pl.ds(0, pairs - 1)], share_out)
    sent(hbuf.at[:, pl.ds(blk, (PLANE - 1) * blk), :], h_send)
    sent(proj, p_send.at[0])
    sent(proj, p_send.at[1])
    sent(bbuf.at[:, :, pl.ds(rows, (PLANE - 1) * rows)], b_send)
    for kind, offsets in (("a1", (0,)), ("a2", (0,)), ("b1", (0, 1, -1, 2)), ("b2", (0, 1, -1, 2))):
        each(kind, offsets, lambda m: m.wait_send())


def on_device(amplitudes, factor, home, domains, coupling, hole_weight, virt_energy, occ_i, occ_j):
    pairs = lax.axis_size("pair")
    ni, rows, width = amplitudes.shape[1:]
    stored, rank = factor.shape
    tiles_here = stored // TILE
    tiles = home.shape[0]
    blk = rank // PLANE
    lines = virt_energy.shape[0] // (2 * TILE)

    f32, bf16, i32 = jnp.float32, jnp.bfloat16, jnp.int32
    dma = pltpu.SemaphoreType.DMA
    chunks = ni // CHUNK
    done = ni - CHUNK
    vmem = pl.BlockSpec(memory_space=pltpu.VMEM)
    smem = pl.BlockSpec(memory_space=pltpu.SMEM)
    hbm = pl.BlockSpec(memory_space=pltpu.HBM)
    held = pl.pallas_call(
        residual_kernel,
        out_shape=(
            pltpu.VMEM((done, rows, width), f32),
            pltpu.VMEM((ni * rows, width), bf16),
            pltpu.VMEM((rank, width), bf16),
            pltpu.VMEM((ni, rank, rows), bf16),
            pltpu.VMEM((1, width), f32),
            pltpu.VMEM((rows, rows), f32),
        ),
        in_specs=[hbm] * 8 + [smem],
        out_specs=(vmem,) * 6,
        scratch_shapes=[
            pltpu.VMEM((tiles_here, TILE, rank), bf16),
            pltpu.VMEM((1, tiles), i32),
            pltpu.VMEM(domains.shape, i32),
            pltpu.VMEM((blk, rank), bf16),
            pltpu.VMEM((3, blk), bf16),
            pltpu.VMEM((lines, 2 * TILE), f32),
            pltpu.SMEM((ni,), f32),
            pltpu.VMEM((8, 128), i32),
            pltpu.SMEM((8, 128), i32),
            pltpu.VMEM((3, blk, 128), f32),
            pltpu.VMEM((pairs, 1, 128), i32),
            pltpu.SMEM((pairs, 1, 128), i32),
            pltpu.VMEM((tiles // 2, PLANE * SHARE // pairs, 2 * TILE), bf16),
            pltpu.VMEM((pairs, PLANE * SHARE // pairs, width), bf16),
            pltpu.VMEM((CAP // 2, rank, 2 * TILE), bf16),
            pltpu.VMEM((PLANE * CAP // 2, 32, 2 * TILE), bf16),
            pltpu.VMEM((PLANE * CAP // 2, blk - SHARE - 32, 2 * TILE), bf16),
            pltpu.VMEM((ni, rank, rows), bf16),
            pltpu.VMEM((ni, blk, width), bf16),
            pltpu.VMEM((ni, blk, rank), bf16),
            pltpu.VMEM((ni, blk, rank), bf16),
            pltpu.VMEM((ni, blk, rank), bf16),
            pltpu.VMEM((CHUNK * blk, rank), bf16),
            pltpu.VMEM((ni, blk, width), bf16),
            dma((8,)),
            dma,
            dma,
            dma,
            dma((4,)),
            dma,
            dma,
            dma,
            dma((2,)),
            dma((40,)),
            dma((40,)),
            dma,
            dma((chunks,)),
            dma((2,)),
            dma((chunks,)),
            dma((chunks,)),
            dma,
            dma((chunks,)),
        ],
        compiler_params=pltpu.CompilerParams(
            collective_id=0, has_side_effects=True, vmem_limit_bytes=40 * 2**20
        ),
    )(
        factor.reshape(tiles_here, TILE, rank),
        home[None, :],
        domains,
        amplitudes.reshape(ni * rows, width),
        coupling,
        hole_weight[0],
        virt_energy.reshape(lines, 2 * TILE),
        occ_i,
        occ_j,
    )
    residual = pl.pallas_call(
        last_kernel,
        out_shape=jax.ShapeDtypeStruct((ni, rows, width), f32),
        in_specs=[smem] + [vmem] * 6,
        out_specs=hbm,
        scratch_shapes=[
            pltpu.VMEM((CHUNK, rows, width), f32),
            dma((done,)),
            dma((len(ladder_steps(width)),)),
        ],
        compiler_params=pltpu.CompilerParams(vmem_limit_bytes=16 * 2**20),
    )(occ_i, *held)
    return residual[None]


def solution(mesh):
    placed = (
        P("pair", None, "virt", None),
        P("virt", None),
        P(),
        P("pair", None),
        P("virt", None),
        P("pair", None, "virt"),
        P(),
        P(),
        P("pair"),
    )
    return jax.shard_map(
        on_device,
        mesh=mesh,
        in_specs=placed,
        out_specs=P("pair", None, "virt", None),
        check_vma=False,
    )
```

```python
import jax
import jax.numpy as jnp
from jax import lax
from jax.experimental import pallas as pl
from jax.experimental.pallas import tpu as pltpu
from jax.sharding import PartitionSpec as P

TILE = 64
CAP = 4
SIDE = 4
PLANE = SIDE * SIDE
CHUNK = 2
SHARE = 16
MESH = pl.DeviceIdType.MESH
NT = (((1,), (1,)), ((), ()))
NN = (((1,), (0,)), ((), ()))


def dot(a, b, dims):
    return lax.dot_general(a, b, dims, preferred_element_type=jnp.float32)


def ladder_steps(width):
    return [slice(b, b + 512) for b in range(0, width, 512)]


def ladder_left(recvb, c):
    return jnp.concatenate([recvb[c * CHUNK + i].T for i in range(CHUNK)], axis=0)


def ladder_part(left, c, cols, dt, amp, col, row, occ_i, out, slot):
    rows = left.shape[0] // CHUNK
    part = dot(left, dt[:, cols], NN)
    for i in range(CHUNK):
        lines = pl.ds(pl.multiple_of((c * CHUNK + i) * rows, rows), rows)
        shift = row[:, :1] + (col[:, cols] - occ_i[c * CHUNK + i])
        out[slot * CHUNK + i, :, cols] = part[i * rows : (i + 1) * rows] + shift * amp[
            lines, cols
        ].astype(jnp.float32)


def last_kernel(occ_i, ladder, amp, dt, recvb, col, row, out_hbm, last, sem, last_sem):
    done = ladder.shape[0]
    c = done // CHUNK
    copies = [pltpu.make_async_copy(ladder.at[i], out_hbm.at[i], sem.at[i]) for i in range(done)]
    for copy in copies:
        copy.start()
    left = ladder_left(recvb, c)
    for k, cols in enumerate(ladder_steps(dt.shape[1])):
        ladder_part(left, c, cols, dt, amp, col, row, occ_i, last, 0)
        copy = pltpu.make_async_copy(
            last.at[:, :, cols], out_hbm.at[pl.ds(done, CHUNK), :, cols], last_sem.at[k]
        )
        copy.start()
        copies.append(copy)
    for copy in copies:
        copy.wait()


def residual_kernel(
    factor_hbm,
    home_hbm,
    domain_hbm,
    amp_hbm,
    coupling_hbm,
    weight_hbm,
    energy_hbm,
    occ_i_hbm,
    occ_j,
    ladder,
    amp,
    dt,
    recvb,
    col,
    row,
    factor,
    home,
    domain,
    coupling,
    weight,
    energy,
    occ_i,
    table,
    where,
    columns,
    all_slots,
    slot_lists,
    full,
    ready,
    pack,
    got_up,
    got_low,
    hbuf,
    recvh,
    proj,
    below,
    above,
    dressed,
    bbuf,
    io_sem,
    slot_send,
    slot_recv,
    full_send,
    full_recv,
    share_out,
    share_in,
    pack_sem,
    got_sem,
    ag_send,
    ag_recv,
    h_send,
    h_recv,
    p_send,
    below_sem,
    above_sem,
    b_send,
    b_recv,
):
    f32, bf16, i32 = jnp.float32, jnp.bfloat16, jnp.int32
    pairs = lax.axis_size("pair")
    pair = lax.axis_index("pair")
    me = lax.axis_index("virt")
    y, x = lax.div(me, SIDE), lax.rem(me, SIDE)
    after = lax.rem(pair + 1, pairs)
    before = lax.rem(pair + pairs - 1, pairs)
    rank, width = dt.shape
    blk = rank // PLANE
    rows = width // PLANE
    chunks = hbuf.shape[0] // CHUNK
    tiles_here = factor.shape[0]
    in_domain = width // TILE

    barrier = pltpu.get_barrier_semaphore()

    @pl.loop(1, PLANE)
    def _(s):
        pl.semaphore_signal(
            barrier, inc=1, device_id=(pair, lax.rem(me + s, PLANE)), device_id_type=MESH
        )

    @pl.loop(1, pairs)
    def _(s):
        pl.semaphore_signal(
            barrier, inc=1, device_id=(lax.rem(pair + s, pairs), me), device_id_type=MESH
        )

    def fetch(k, src, dst):
        copy = pltpu.make_async_copy(src, dst, io_sem.at[k])
        copy.start()
        return copy

    get_home = fetch(0, home_hbm, home)
    get_domain = fetch(1, domain_hbm, domain)
    get_factor = fetch(2, factor_hbm, factor)
    get_small = [
        fetch(3, coupling_hbm, coupling),
        fetch(4, weight_hbm, weight),
        fetch(5, energy_hbm, energy),
        fetch(6, occ_i_hbm, occ_i),
    ]
    get_amp = fetch(7, amp_hbm, amp)

    get_home.wait()
    get_domain.wait()
    tiles = home.shape[1]
    home_row = jnp.broadcast_to(home[...], (in_domain, tiles))
    domain_row = jnp.broadcast_to(domain[...], (tiles, in_domain))
    slots = lax.broadcasted_iota(i32, (in_domain, tiles), 1)
    slot_col = jnp.max(jnp.where(home_row == domain_row.T, slots, 0), axis=1, keepdims=True)
    slots = lax.broadcasted_iota(i32, (tiles, in_domain), 0)
    slot_row = jnp.max(jnp.where(home_row.T == domain_row, slots, 0), axis=0, keepdims=True)
    holder_col, holder_row = lax.div(slot_col, tiles_here), lax.div(slot_row, tiles_here)
    same = holder_col == holder_row
    up = lax.broadcasted_iota(i32, (in_domain, in_domain), 0)
    across = lax.broadcasted_iota(i32, (in_domain, in_domain), 1)
    nth_row = jnp.sum(jnp.where(same & (up < across), 1, 0), axis=0, keepdims=True)
    nth_col = jnp.sum(jnp.where(same & (across < up), 1, 0), axis=1, keepdims=True)
    nth_row, nth_col = jnp.minimum(nth_row, CAP - 1), jnp.minimum(nth_col, CAP - 1)
    number = lax.broadcasted_iota(i32, (in_domain, 128), 1)
    mine = jnp.max(
        jnp.where(
            (holder_col == me) & (nth_col == number), lax.rem(slot_col, tiles_here), 0
        ),
        axis=0,
        keepdims=True,
    )
    table[0:1, 0:in_domain] = holder_row * (CAP // 2) + lax.div(nth_row, 2)
    table[1:2, 0:in_domain] = lax.rem(nth_row, 2)
    table[2:3, 0:in_domain] = lax.div(domain[...], 2)
    table[3:4, 0:in_domain] = lax.rem(domain[...], 2)
    table[4:5, :] = mine
    table[5:8, :] = jnp.zeros((3, 128), i32)
    scalars = fetch(0, table, where)
    all_slots[pair] = jnp.zeros((1, 128), i32)
    turn = lax.rem(slot_row + lax.broadcasted_iota(i32, (1, in_domain), 1), 2)
    all_slots[pair, :, 0:in_domain] = lax.div(slot_row, 2) + turn * (tiles // 2)
    scalars.wait()

    get_factor.wait()
    for c in range(CAP // 2):
        two = jnp.concatenate([factor[where[4, 2 * c]], factor[where[4, 2 * c + 1]]], axis=0)
        pack[c] = two.T

    keep = blk - SHARE
    per = PLANE // pairs
    rank_cols = pl.ds(pl.multiple_of(pair * per * blk, per * blk), per * blk)
    wide = factor[:, :, rank_cols].reshape(tiles_here * TILE, per * blk).T
    wide = jnp.concatenate([wide[k * blk + keep : (k + 1) * blk] for k in range(per)], axis=0)
    two_here = tiles_here // 2
    for k in range(two_here):
        full[me * two_here + k] = wide[:, k * 2 * TILE : (k + 1) * 2 * TILE]

    pl.semaphore_wait(barrier, PLANE + pairs - 2)

    hs = per * SHARE // 2

    @pl.loop(1, pairs)
    def _(s):
        pltpu.make_async_remote_copy(
            all_slots.at[pair], all_slots.at[pair], slot_send, slot_recv,
            device_id=(lax.rem(pair + s, pairs), me), device_id_type=MESH,
        ).start()

    def share_send(first, n, h, sem, to):
        part = full.at[pl.ds(first, n), h * hs : (h + 1) * hs, :]
        pltpu.make_async_remote_copy(
            part, part, full_send, full_recv.at[sem], device_id=(pair, to), device_id_type=MESH
        ).start()

    def to_x(s):
        return y * SIDE + lax.rem(x + s, SIDE)

    def to_y(s):
        return lax.rem(y + s, SIDE) * SIDE + x

    for s in range(1, SIDE):
        share_send(me * two_here, two_here, 0, 0, to_x(s))
        share_send(me * two_here, two_here, 1, 1, to_y(s))

    got = (got_up, got_low)
    offs = (0, got_up.shape[1])

    def pack_part(d, h):
        return pack.at[:, pl.ds(pl.multiple_of(d * blk + offs[h], 16), got[h].shape[1]), :]

    for h in range(2):
        here = got[h].at[pl.ds(me * (CAP // 2), CAP // 2)]

        @pl.loop(1, PLANE)
        def _(s):
            d = lax.rem(me + s, PLANE)
            pltpu.make_async_remote_copy(
                pack_part(d, h), here, pack_sem, got_sem.at[h],
                device_id=(pair, d), device_id_type=MESH,
            ).start()

        pltpu.make_async_copy(pack_part(me, h), here, got_sem.at[h]).start()

    def share_landed(n, h, sem):
        part = full.at[pl.ds(0, n), h * hs : (h + 1) * hs, :]
        pltpu.make_async_copy(part, part, full_recv.at[sem]).wait()

    share_landed((SIDE - 1) * two_here, 0, 0)
    for s in range(1, SIDE):
        share_send(y * SIDE * two_here, SIDE * two_here, 0, 2, to_y(s))
    share_landed((SIDE - 1) * two_here, 1, 1)
    for s in range(1, SIDE):
        for k in range(SIDE):
            share_send((k * SIDE + x) * two_here, two_here, 1, 3, to_x(s))

    for copy in get_small:
        copy.wait()

    def halves(wide, second):
        return jnp.where(second == 1, wide[:, TILE:], wide[:, :TILE])

    low = lax.broadcasted_iota(i32, (32, 2 * TILE), 1) < TILE

    def swapped(wide):
        return jnp.concatenate([wide[:, TILE:], wide[:, :TILE]], axis=1)

    def energy_of(t):
        return halves(energy[pl.ds(where[2, t], 1), :], where[3, t])

    for u in range(in_domain // 2):
        col[:, u * 2 * TILE : (u + 1) * 2 * TILE] = jnp.concatenate(
            [energy_of(2 * u), energy_of(2 * u + 1)], axis=1
        )
    here_energy = col[:, pl.ds(pl.multiple_of(me * rows, rows), rows)]
    row[...] = jnp.broadcast_to(here_energy, (rows, rows)).T - occ_j[0]
    has = (jnp.where(pair > 0, 1.0, 0.0), 1.0, jnp.where(pair < pairs - 1, 1.0, 0.0))
    for d in range(3):
        line = weight[d : d + 1, :].astype(f32) * has[d]
        columns[d] = jnp.broadcast_to(line, (128, blk)).T

    own = pl.ds(pl.multiple_of(me * blk, blk), blk)

    def arrange(h):
        pltpu.make_async_copy(got[h], got[h], got_sem.at[h]).wait()
        lines = pl.ds(pl.multiple_of(me * blk + offs[h], 16), got[h].shape[1])
        for u in range(in_domain // 2):
            even, odd = [
                jnp.where(where[1, t] == t % 2, wide, swapped(wide))
                for t in (2 * u, 2 * u + 1)
                for wide in (got[h][where[0, t]],)
            ]
            dt[lines, u * 2 * TILE : (u + 1) * 2 * TILE] = jnp.where(
                low[: even.shape[0]], even, odd
            )

    def device(dy, dx):
        return lax.rem(y + dy + SIDE, SIDE) * SIDE + lax.rem(x + dx + SIDE, SIDE)

    def at(axis, along, other):
        return device(other, along) if axis == 0 else device(along, other)

    names = {}

    def message(kind, h, s, sign):
        k = names.setdefault((kind, h, s, sign), len(names))
        if kind == "a1":
            block, to = at(h, 0, 0), at(h, sign, 0)
        elif kind == "a2":
            block, to = at(h, -sign, 0), at(h, sign, 0)
        elif kind == "b1":
            block, to = at(h, s, 0), at(h, 0, sign)
        else:
            block, to = at(h, s, -sign), at(h, 0, sign)
        if kind in ("a1", "b1"):
            off, n = h * (width // 2), width // 2
        else:
            off, n = h * (width // 2) + (0 if sign > 0 else width // 4), width // 4
        part = dt.at[pl.ds(pl.multiple_of(block * blk, blk), keep), off : off + n]
        return pltpu.make_async_remote_copy(
            part, part, ag_send.at[k], ag_recv.at[k], device_id=(pair, to), device_id_type=MESH
        )

    def each(kind, offsets, do):
        for s in offsets:
            for h in (0, 1):
                for sign in (1, -1):
                    do(message(kind, h, s, sign))

    def go(m):
        m.start()

    def landed(m):
        m.wait_recv()

    def send(src, dst, send_sem, recv_sem, d):
        @pl.when(d != me)
        def _():
            pltpu.make_async_remote_copy(
                src, dst, send_sem, recv_sem, device_id=(pair, d), device_id_type=MESH
            ).start()

        @pl.when(d == me)
        def _():
            pltpu.make_async_copy(src, dst, recv_sem).start()

    def band_of(d):
        return pl.ds(pl.multiple_of(d * blk, blk), blk)

    def half(c, r):
        now = pl.ds(c * CHUNK, CHUNK)
        band = pl.ds(pl.multiple_of(r * SIDE * blk, SIDE * blk), SIDE * blk)
        lines = pl.ds(pl.multiple_of(c * CHUNK * rows, CHUNK * rows), CHUNK * rows)
        part = dot(dt[band, :], amp[lines, :], NT).astype(bf16)
        for i in range(CHUNK):
            hbuf[c * CHUNK + i, band, :] = part[:, i * rows : (i + 1) * rows]
        for w in range(SIDE):
            d = r * SIDE + lax.rem(x + w, SIDE)
            send(
                hbuf.at[now, band_of(d), :],
                recvh.at[now, :, pl.ds(pl.multiple_of(me * rows, rows), rows)],
                h_send,
                h_recv.at[c],
                d,
            )

    arrange(0)
    arrange(1)
    each("a1", (0,), go)
    each("b1", (0,), go)

    pltpu.make_async_copy(
        all_slots.at[pl.ds(0, pairs - 1)], all_slots.at[pl.ds(0, pairs - 1)], slot_recv
    ).wait()
    lists = fetch(0, all_slots, slot_lists)
    share_landed((SIDE - 1) * SIDE * two_here, 0, 2)
    share_landed((SIDE - 1) * SIDE * two_here, 1, 3)
    for k in range(tiles // 2):
        full[tiles // 2 + k] = swapped(full[k])
    lists.wait()

    def hand_out(first, last):
        @pl.loop(first, last)
        def _(k):
            p = lax.rem(pair + pairs // 2 + k, pairs)

            for u in range(in_domain // 2):
                ready[p, :, u * 2 * TILE : (u + 1) * 2 * TILE] = jnp.where(
                    low, full[slot_lists[p, 0, 2 * u]], full[slot_lists[p, 0, 2 * u + 1]]
                )

            for b in range(per):
                src = ready.at[p, b * SHARE : (b + 1) * SHARE, :]
                start = pl.multiple_of((pair * per + b) * blk + keep, SHARE)
                dst = dt.at[pl.ds(start, SHARE), :]

                @pl.when(p != pair)
                def _():
                    pltpu.make_async_remote_copy(
                        src, dst, share_out, share_in, device_id=(p, me), device_id_type=MESH
                    ).start()

                @pl.when(p == pair)
                def _():
                    pltpu.make_async_copy(src, dst, share_in).start()

    hand_out(0, 3)
    for h in (0, 1):
        for sign in (1, -1):
            message("a1", h, 0, sign).wait_recv()
            message("a2", h, 0, sign).start()
    each("b1", (1, -1), go)
    hand_out(3, 5)
    each("b1", (0,), landed)
    each("b2", (0,), go)
    each("a2", (0,), landed)
    each("b1", (2,), go)
    hand_out(5, pairs)
    each("b2", (0,), landed)
    each("b1", (1, -1), landed)
    each("b2", (1, -1), go)
    each("b1", (2,), landed)
    each("b2", (2,), go)

    each("b2", (1, -1, 2), landed)
    all_shares = dt.at[pl.ds(0, PLANE * SHARE), :]
    pltpu.make_async_copy(all_shares, all_shares, share_in).wait()
    get_amp.wait()

    @pl.loop(0, chunks)
    def _(c):
        @pl.loop(0, SIDE)
        def _(k):
            half(c, lax.rem(y + k, SIDE))

    def project(c):
        now = pl.ds(c * CHUNK, CHUNK)
        pltpu.make_async_copy(recvh.at[now], recvh.at[now], h_recv.at[c]).wait()
        left = recvh[now].reshape(CHUNK * blk, width)
        step = 256
        for n in range(rank // step):
            cols = slice(n * step, (n + 1) * step)
            part = dot(left, dt[cols, :], NT).astype(bf16)
            proj[now, :, cols] = part.reshape(CHUNK, blk, step)
        pltpu.make_async_remote_copy(
            proj.at[now], below.at[now], p_send.at[0], below_sem.at[c],
            device_id=(after, me), device_id_type=MESH,
        ).start()
        pltpu.make_async_remote_copy(
            proj.at[now], above.at[now], p_send.at[1], above_sem.at[c],
            device_id=(before, me), device_id_type=MESH,
        ).start()

    def finish(c):
        now = pl.ds(c * CHUNK, CHUNK)
        pltpu.make_async_copy(below.at[now], below.at[now], below_sem.at[c]).wait()
        pltpu.make_async_copy(above.at[now], above.at[now], above_sem.at[c]).wait()
        for i in range(CHUNK):
            mid = proj[c * CHUNK + i].astype(f32)
            hole = (
                columns[0][:, :1] * below[c * CHUNK + i].astype(f32)
                + columns[1][:, :1] * mid
                + columns[2][:, :1] * above[c * CHUNK + i].astype(f32)
            )
            dressed[i * blk : (i + 1) * blk, :] = (
                coupling[...].astype(f32) * mid + hole
            ).astype(bf16)

        @pl.loop(0, SIDE)
        def _(k):
            r = lax.rem(y + k, SIDE)
            cols = pl.ds(pl.multiple_of(r * SIDE * rows, SIDE * rows), SIDE * rows)
            part = dot(dressed[...], dt[:, cols], NN).astype(bf16)
            bbuf[now, :, cols] = part.reshape(CHUNK, blk, SIDE * rows)
            for w in range(SIDE):
                d = r * SIDE + lax.rem(x + w, SIDE)
                src = bbuf.at[now, :, pl.ds(pl.multiple_of(d * rows, rows), rows)]
                send(src, recvb.at[now, own, :], b_send, b_recv.at[c], d)

    @pl.loop(0, chunks + 1)
    def _(c):
        @pl.when(c < chunks)
        def _():
            project(c)

        @pl.when(c > 0)
        def _():
            finish(c - 1)

    @pl.loop(0, chunks)
    def _(c):
        now = pl.ds(c * CHUNK, CHUNK)
        pltpu.make_async_copy(recvb.at[now], recvb.at[now], b_recv.at[c]).wait()

        @pl.when(c < chunks - 1)
        def _():
            left = ladder_left(recvb, c)
            for cols in ladder_steps(width):
                ladder_part(left, c, cols, dt, amp, col, row, occ_i, ladder, c)

    def sent(ref, sem):
        pltpu.make_async_copy(ref, ref, sem).wait()

    sent(pack.at[:, pl.ds(0, (PLANE - 1) * keep), :], pack_sem)
    sent(all_slots.at[pl.ds(0, pairs - 1)], slot_send)
    units = (SIDE - 1) * (2 + 2 * SIDE) * two_here
    sent(full.at[pl.ds(0, units // 2)], full_send)
    sent(ready.at[pl.ds(0, pairs - 1)], share_out)
    sent(hbuf.at[:, pl.ds(blk, (PLANE - 1) * blk), :], h_send)
    sent(proj, p_send.at[0])
    sent(proj, p_send.at[1])
    sent(bbuf.at[:, :, pl.ds(rows, (PLANE - 1) * rows)], b_send)
    for kind, offsets in (("a1", (0,)), ("a2", (0,)), ("b1", (0, 1, -1, 2)), ("b2", (0, 1, -1, 2))):
        each(kind, offsets, lambda m: m.wait_send())


def on_device(amplitudes, factor, home, domains, coupling, hole_weight, virt_energy, occ_i, occ_j):
    pairs = lax.axis_size("pair")
    ni, rows, width = amplitudes.shape[1:]
    stored, rank = factor.shape
    tiles_here = stored // TILE
    tiles = home.shape[0]
    blk = rank // PLANE
    lines = virt_energy.shape[0] // (2 * TILE)

    f32, bf16, i32 = jnp.float32, jnp.bfloat16, jnp.int32
    dma = pltpu.SemaphoreType.DMA
    chunks = ni // CHUNK
    done = ni - CHUNK
    vmem = pl.BlockSpec(memory_space=pltpu.VMEM)
    smem = pl.BlockSpec(memory_space=pltpu.SMEM)
    hbm = pl.BlockSpec(memory_space=pltpu.HBM)
    held = pl.pallas_call(
        residual_kernel,
        out_shape=(
            pltpu.VMEM((done, rows, width), f32),
            pltpu.VMEM((ni * rows, width), bf16),
            pltpu.VMEM((rank, width), bf16),
            pltpu.VMEM((ni, rank, rows), bf16),
            pltpu.VMEM((1, width), f32),
            pltpu.VMEM((rows, rows), f32),
        ),
        in_specs=[hbm] * 8 + [smem],
        out_specs=(vmem,) * 6,
        scratch_shapes=[
            pltpu.VMEM((tiles_here, TILE, rank), bf16),
            pltpu.VMEM((1, tiles), i32),
            pltpu.VMEM(domains.shape, i32),
            pltpu.VMEM((blk, rank), bf16),
            pltpu.VMEM((3, blk), bf16),
            pltpu.VMEM((lines, 2 * TILE), f32),
            pltpu.SMEM((ni,), f32),
            pltpu.VMEM((8, 128), i32),
            pltpu.SMEM((8, 128), i32),
            pltpu.VMEM((3, blk, 128), f32),
            pltpu.VMEM((pairs, 1, 128), i32),
            pltpu.SMEM((pairs, 1, 128), i32),
            pltpu.VMEM((tiles, PLANE * SHARE // pairs, 2 * TILE), bf16),
            pltpu.VMEM((pairs, PLANE * SHARE // pairs, width), bf16),
            pltpu.VMEM((CAP // 2, rank, 2 * TILE), bf16),
            pltpu.VMEM((PLANE * CAP // 2, 32, 2 * TILE), bf16),
            pltpu.VMEM((PLANE * CAP // 2, blk - SHARE - 32, 2 * TILE), bf16),
            pltpu.VMEM((ni, rank, rows), bf16),
            pltpu.VMEM((ni, blk, width), bf16),
            pltpu.VMEM((ni, blk, rank), bf16),
            pltpu.VMEM((ni, blk, rank), bf16),
            pltpu.VMEM((ni, blk, rank), bf16),
            pltpu.VMEM((CHUNK * blk, rank), bf16),
            pltpu.VMEM((ni, blk, width), bf16),
            dma((8,)),
            dma,
            dma,
            dma,
            dma((4,)),
            dma,
            dma,
            dma,
            dma((2,)),
            dma((40,)),
            dma((40,)),
            dma,
            dma((chunks,)),
            dma((2,)),
            dma((chunks,)),
            dma((chunks,)),
            dma,
            dma((chunks,)),
        ],
        compiler_params=pltpu.CompilerParams(
            collective_id=0, has_side_effects=True, vmem_limit_bytes=40 * 2**20
        ),
    )(
        factor.reshape(tiles_here, TILE, rank),
        home[None, :],
        domains,
        amplitudes.reshape(ni * rows, width),
        coupling,
        hole_weight[0],
        virt_energy.reshape(lines, 2 * TILE),
        occ_i,
        occ_j,
    )
    residual = pl.pallas_call(
        last_kernel,
        out_shape=jax.ShapeDtypeStruct((ni, rows, width), f32),
        in_specs=[smem] + [vmem] * 6,
        out_specs=hbm,
        scratch_shapes=[
            pltpu.VMEM((CHUNK, rows, width), f32),
            dma((done,)),
            dma((len(ladder_steps(width)),)),
        ],
        compiler_params=pltpu.CompilerParams(vmem_limit_bytes=16 * 2**20),
    )(occ_i, *held)
    return residual[None]


def solution(mesh):
    placed = (
        P("pair", None, "virt", None),
        P("virt", None),
        P(),
        P("pair", None),
        P("virt", None),
        P("pair", None, "virt"),
        P(),
        P(),
        P("pair"),
    )
    return jax.shard_map(
        on_device,
        mesh=mesh,
        in_specs=placed,
        out_specs=P("pair", None, "virt", None),
        check_vma=False,
    )
```

```python
import jax
import jax.numpy as jnp
from jax import lax
from jax.experimental import pallas as pl
from jax.experimental.pallas import tpu as pltpu
from jax.sharding import PartitionSpec as P

TILE = 64
CAP = 4
SIDE = 4
PLANE = SIDE * SIDE
CHUNK = 2
SHARE = 16
MESH = pl.DeviceIdType.MESH
NT = (((1,), (1,)), ((), ()))
NN = (((1,), (0,)), ((), ()))


def dot(a, b, dims):
    return lax.dot_general(a, b, dims, preferred_element_type=jnp.float32)


def ladder_steps(width):
    return [slice(b, b + 512) for b in range(0, width, 512)]


def ladder_left(recvb, c):
    return jnp.concatenate([recvb[c * CHUNK + i].T for i in range(CHUNK)], axis=0)


def ladder_part(left, c, cols, dt, amp, col, row, occ_i, out, slot):
    rows = left.shape[0] // CHUNK
    part = dot(left, dt[:, cols], NN)
    for i in range(CHUNK):
        lines = pl.ds(pl.multiple_of((c * CHUNK + i) * rows, rows), rows)
        shift = row[:, :1] + (col[:, cols] - occ_i[c * CHUNK + i])
        out[slot * CHUNK + i, :, cols] = part[i * rows : (i + 1) * rows] + shift * amp[
            lines, cols
        ].astype(jnp.float32)


def last_kernel(occ_i, ladder, amp, dt, recvb, col, row, out_hbm, last, sem, last_sem):
    done = ladder.shape[0]
    c = done // CHUNK
    copies = [pltpu.make_async_copy(ladder.at[i], out_hbm.at[i], sem.at[i]) for i in range(done)]
    for copy in copies:
        copy.start()
    left = ladder_left(recvb, c)
    for k, cols in enumerate(ladder_steps(dt.shape[1])):
        ladder_part(left, c, cols, dt, amp, col, row, occ_i, last, 0)
        copy = pltpu.make_async_copy(
            last.at[:, :, cols], out_hbm.at[pl.ds(done, CHUNK), :, cols], last_sem.at[k]
        )
        copy.start()
        copies.append(copy)
    for copy in copies:
        copy.wait()


def residual_kernel(
    factor_hbm,
    home_hbm,
    domain_hbm,
    amp_hbm,
    coupling_hbm,
    weight_hbm,
    energy_hbm,
    occ_i_hbm,
    occ_j,
    ladder,
    amp,
    dt,
    recvb,
    col,
    row,
    factor,
    home,
    domain,
    coupling,
    weight,
    energy,
    occ_i,
    table,
    where,
    columns,
    all_slots,
    slot_lists,
    full,
    ready,
    pack,
    got_up,
    hbuf,
    recvh,
    proj,
    below,
    above,
    dressed,
    bbuf,
    io_sem,
    slot_send,
    slot_recv,
    full_send,
    full_recv,
    share_out,
    share_in,
    pack_sem,
    got_sem,
    ag_send,
    ag_recv,
    h_send,
    h_recv,
    p_send,
    below_sem,
    above_sem,
    b_send,
    b_recv,
):
    f32, bf16, i32 = jnp.float32, jnp.bfloat16, jnp.int32
    pairs = lax.axis_size("pair")
    pair = lax.axis_index("pair")
    me = lax.axis_index("virt")
    y, x = lax.div(me, SIDE), lax.rem(me, SIDE)
    after = lax.rem(pair + 1, pairs)
    before = lax.rem(pair + pairs - 1, pairs)
    rank, width = dt.shape
    blk = rank // PLANE
    rows = width // PLANE
    chunks = hbuf.shape[0] // CHUNK
    tiles_here = factor.shape[0]
    in_domain = width // TILE

    barrier = pltpu.get_barrier_semaphore()

    @pl.loop(1, PLANE)
    def _(s):
        pl.semaphore_signal(
            barrier, inc=1, device_id=(pair, lax.rem(me + s, PLANE)), device_id_type=MESH
        )

    @pl.loop(1, pairs)
    def _(s):
        pl.semaphore_signal(
            barrier, inc=1, device_id=(lax.rem(pair + s, pairs), me), device_id_type=MESH
        )

    def fetch(k, src, dst):
        copy = pltpu.make_async_copy(src, dst, io_sem.at[k])
        copy.start()
        return copy

    get_home = fetch(0, home_hbm, home)
    get_domain = fetch(1, domain_hbm, domain)
    get_factor = fetch(2, factor_hbm, factor)
    get_small = [
        fetch(3, coupling_hbm, coupling),
        fetch(4, weight_hbm, weight),
        fetch(5, energy_hbm, energy),
        fetch(6, occ_i_hbm, occ_i),
    ]
    get_amp = fetch(7, amp_hbm, amp)

    get_home.wait()
    get_domain.wait()
    tiles = home.shape[1]
    home_row = jnp.broadcast_to(home[...], (in_domain, tiles))
    domain_row = jnp.broadcast_to(domain[...], (tiles, in_domain))
    slots = lax.broadcasted_iota(i32, (in_domain, tiles), 1)
    slot_col = jnp.max(jnp.where(home_row == domain_row.T, slots, 0), axis=1, keepdims=True)
    slots = lax.broadcasted_iota(i32, (tiles, in_domain), 0)
    slot_row = jnp.max(jnp.where(home_row.T == domain_row, slots, 0), axis=0, keepdims=True)
    holder_col, holder_row = lax.div(slot_col, tiles_here), lax.div(slot_row, tiles_here)
    same = holder_col == holder_row
    up = lax.broadcasted_iota(i32, (in_domain, in_domain), 0)
    across = lax.broadcasted_iota(i32, (in_domain, in_domain), 1)
    nth_row = jnp.sum(jnp.where(same & (up < across), 1, 0), axis=0, keepdims=True)
    nth_col = jnp.sum(jnp.where(same & (across < up), 1, 0), axis=1, keepdims=True)
    nth_row, nth_col = jnp.minimum(nth_row, CAP - 1), jnp.minimum(nth_col, CAP - 1)
    number = lax.broadcasted_iota(i32, (in_domain, 128), 1)
    mine = jnp.max(
        jnp.where(
            (holder_col == me) & (nth_col == number), lax.rem(slot_col, tiles_here), 0
        ),
        axis=0,
        keepdims=True,
    )
    table[0:1, 0:in_domain] = holder_row * (CAP // 2) + lax.div(nth_row, 2)
    table[1:2, 0:in_domain] = lax.rem(nth_row, 2)
    table[2:3, 0:in_domain] = lax.div(domain[...], 2)
    table[3:4, 0:in_domain] = lax.rem(domain[...], 2)
    table[4:5, :] = mine
    table[5:8, :] = jnp.zeros((3, 128), i32)
    scalars = fetch(0, table, where)
    all_slots[pair] = jnp.zeros((1, 128), i32)
    turn = lax.rem(slot_row + lax.broadcasted_iota(i32, (1, in_domain), 1), 2)
    all_slots[pair, :, 0:in_domain] = lax.div(slot_row, 2) + turn * (tiles // 2)
    scalars.wait()

    get_factor.wait()
    for c in range(CAP // 2):
        two = jnp.concatenate([factor[where[4, 2 * c]], factor[where[4, 2 * c + 1]]], axis=0)
        pack[c] = two.T

    keep = blk - SHARE
    per = PLANE // pairs
    rank_cols = pl.ds(pl.multiple_of(pair * per * blk, per * blk), per * blk)
    wide = factor[:, :, rank_cols].reshape(tiles_here * TILE, per * blk).T
    wide = jnp.concatenate([wide[k * blk + keep : (k + 1) * blk] for k in range(per)], axis=0)
    two_here = tiles_here // 2
    for k in range(two_here):
        full[me * two_here + k] = wide[:, k * 2 * TILE : (k + 1) * 2 * TILE]

    pl.semaphore_wait(barrier, PLANE + pairs - 2)

    hs = per * SHARE // 2

    @pl.loop(1, pairs)
    def _(s):
        pltpu.make_async_remote_copy(
            all_slots.at[pair], all_slots.at[pair], slot_send, slot_recv,
            device_id=(lax.rem(pair + s, pairs), me), device_id_type=MESH,
        ).start()

    def share_send(first, n, h, sem, to):
        part = full.at[pl.ds(first, n), h * hs : (h + 1) * hs, :]
        pltpu.make_async_remote_copy(
            part, part, full_send, full_recv.at[sem], device_id=(pair, to), device_id_type=MESH
        ).start()

    def to_x(s):
        return y * SIDE + lax.rem(x + s, SIDE)

    def to_y(s):
        return lax.rem(y + s, SIDE) * SIDE + x

    for s in range(1, SIDE):
        share_send(me * two_here, two_here, 0, 0, to_x(s))
        share_send(me * two_here, two_here, 1, 1, to_y(s))

    got = (got_up,)
    offs = (0,)

    def pack_part(d, h):
        return pack.at[:, pl.ds(pl.multiple_of(d * blk + offs[h], 16), got[h].shape[1]), :]

    for h in range(1):
        here = got[h].at[pl.ds(me * (CAP // 2), CAP // 2)]

        @pl.loop(1, PLANE)
        def _(s):
            d = lax.rem(me + s, PLANE)
            pltpu.make_async_remote_copy(
                pack_part(d, h), here, pack_sem, got_sem.at[h],
                device_id=(pair, d), device_id_type=MESH,
            ).start()

        pltpu.make_async_copy(pack_part(me, h), here, got_sem.at[h]).start()

    def share_landed(n, h, sem):
        part = full.at[pl.ds(0, n), h * hs : (h + 1) * hs, :]
        pltpu.make_async_copy(part, part, full_recv.at[sem]).wait()

    share_landed((SIDE - 1) * two_here, 0, 0)
    for s in range(1, SIDE):
        share_send(y * SIDE * two_here, SIDE * two_here, 0, 2, to_y(s))
    share_landed((SIDE - 1) * two_here, 1, 1)
    for s in range(1, SIDE):
        for k in range(SIDE):
            share_send((k * SIDE + x) * two_here, two_here, 1, 3, to_x(s))

    for copy in get_small:
        copy.wait()

    def halves(wide, second):
        return jnp.where(second == 1, wide[:, TILE:], wide[:, :TILE])

    low = lax.broadcasted_iota(i32, (blk, 2 * TILE), 1) < TILE

    def swapped(wide):
        return jnp.concatenate([wide[:, TILE:], wide[:, :TILE]], axis=1)

    def energy_of(t):
        return halves(energy[pl.ds(where[2, t], 1), :], where[3, t])

    for u in range(in_domain // 2):
        col[:, u * 2 * TILE : (u + 1) * 2 * TILE] = jnp.concatenate(
            [energy_of(2 * u), energy_of(2 * u + 1)], axis=1
        )
    here_energy = col[:, pl.ds(pl.multiple_of(me * rows, rows), rows)]
    row[...] = jnp.broadcast_to(here_energy, (rows, rows)).T - occ_j[0]
    has = (jnp.where(pair > 0, 1.0, 0.0), 1.0, jnp.where(pair < pairs - 1, 1.0, 0.0))
    for d in range(3):
        line = weight[d : d + 1, :].astype(f32) * has[d]
        columns[d] = jnp.broadcast_to(line, (128, blk)).T

    own = pl.ds(pl.multiple_of(me * blk, blk), blk)

    def arrange(h):
        pltpu.make_async_copy(got[h], got[h], got_sem.at[h]).wait()
        lines = pl.ds(pl.multiple_of(me * blk + offs[h], 16), got[h].shape[1])
        for u in range(in_domain // 2):
            even, odd = [
                jnp.where(where[1, t] == t % 2, wide, swapped(wide))
                for t in (2 * u, 2 * u + 1)
                for wide in (got[h][where[0, t]],)
            ]
            dt[lines, u * 2 * TILE : (u + 1) * 2 * TILE] = jnp.where(
                low[: even.shape[0]], even, odd
            )

    def device(dy, dx):
        return lax.rem(y + dy + SIDE, SIDE) * SIDE + lax.rem(x + dx + SIDE, SIDE)

    def at(axis, along, other):
        return device(other, along) if axis == 0 else device(along, other)

    names = {}

    def message(kind, h, s, sign):
        k = names.setdefault((kind, h, s, sign), len(names))
        if kind == "a1":
            block, to = at(h, 0, 0), at(h, sign, 0)
        elif kind == "a2":
            block, to = at(h, -sign, 0), at(h, sign, 0)
        elif kind == "b1":
            block, to = at(h, s, 0), at(h, 0, sign)
        else:
            block, to = at(h, s, -sign), at(h, 0, sign)
        if kind in ("a1", "b1"):
            off, n = h * (width // 2), width // 2
        else:
            off, n = h * (width // 2) + (0 if sign > 0 else width // 4), width // 4
        part = dt.at[pl.ds(pl.multiple_of(block * blk, blk), keep), off : off + n]
        return pltpu.make_async_remote_copy(
            part, part, ag_send.at[k], ag_recv.at[k], device_id=(pair, to), device_id_type=MESH
        )

    def each(kind, offsets, do):
        for s in offsets:
            for h in (0, 1):
                for sign in (1, -1):
                    do(message(kind, h, s, sign))

    def go(m):
        m.start()

    def landed(m):
        m.wait_recv()

    def send(src, dst, send_sem, recv_sem, d):
        @pl.when(d != me)
        def _():
            pltpu.make_async_remote_copy(
                src, dst, send_sem, recv_sem, device_id=(pair, d), device_id_type=MESH
            ).start()

        @pl.when(d == me)
        def _():
            pltpu.make_async_copy(src, dst, recv_sem).start()

    def band_of(d):
        return pl.ds(pl.multiple_of(d * blk, blk), blk)

    def half(c, r):
        now = pl.ds(c * CHUNK, CHUNK)
        band = pl.ds(pl.multiple_of(r * SIDE * blk, SIDE * blk), SIDE * blk)
        lines = pl.ds(pl.multiple_of(c * CHUNK * rows, CHUNK * rows), CHUNK * rows)
        part = dot(dt[band, :], amp[lines, :], NT).astype(bf16)
        for i in range(CHUNK):
            hbuf[c * CHUNK + i, band, :] = part[:, i * rows : (i + 1) * rows]
        for w in range(SIDE):
            d = r * SIDE + lax.rem(x + w, SIDE)
            send(
                hbuf.at[now, band_of(d), :],
                recvh.at[now, :, pl.ds(pl.multiple_of(me * rows, rows), rows)],
                h_send,
                h_recv.at[c],
                d,
            )

    arrange(0)
    each("a1", (0,), go)
    each("b1", (0,), go)

    pltpu.make_async_copy(
        all_slots.at[pl.ds(0, pairs - 1)], all_slots.at[pl.ds(0, pairs - 1)], slot_recv
    ).wait()
    lists = fetch(0, all_slots, slot_lists)
    share_landed((SIDE - 1) * SIDE * two_here, 0, 2)
    share_landed((SIDE - 1) * SIDE * two_here, 1, 3)
    for k in range(tiles // 2):
        full[tiles // 2 + k] = swapped(full[k])
    lists.wait()

    def hand_out(first, last):
        @pl.loop(first, last)
        def _(k):
            p = lax.rem(pair + pairs // 2 + k, pairs)

            for u in range(in_domain // 2):
                ready[p, :, u * 2 * TILE : (u + 1) * 2 * TILE] = jnp.where(
                    low[: full.shape[1]],
                    full[slot_lists[p, 0, 2 * u]],
                    full[slot_lists[p, 0, 2 * u + 1]],
                )

            for b in range(per):
                src = ready.at[p, b * SHARE : (b + 1) * SHARE, :]
                start = pl.multiple_of((pair * per + b) * blk + keep, SHARE)
                dst = dt.at[pl.ds(start, SHARE), :]

                @pl.when(p != pair)
                def _():
                    pltpu.make_async_remote_copy(
                        src, dst, share_out, share_in, device_id=(p, me), device_id_type=MESH
                    ).start()

                @pl.when(p == pair)
                def _():
                    pltpu.make_async_copy(src, dst, share_in).start()

    hand_out(0, 3)
    for h in (0, 1):
        for sign in (1, -1):
            message("a1", h, 0, sign).wait_recv()
            message("a2", h, 0, sign).start()
    each("b1", (1, -1), go)
    hand_out(3, 5)
    each("b1", (0,), landed)
    each("b2", (0,), go)
    each("a2", (0,), landed)
    each("b1", (2,), go)
    hand_out(5, pairs)
    each("b2", (0,), landed)
    each("b1", (1, -1), landed)
    each("b2", (1, -1), go)
    each("b1", (2,), landed)
    each("b2", (2,), go)

    each("b2", (1, -1, 2), landed)
    all_shares = dt.at[pl.ds(0, PLANE * SHARE), :]
    pltpu.make_async_copy(all_shares, all_shares, share_in).wait()
    get_amp.wait()

    @pl.loop(0, chunks)
    def _(c):
        @pl.loop(0, SIDE)
        def _(k):
            half(c, lax.rem(y + k + 1, SIDE))

    def project(c):
        now = pl.ds(c * CHUNK, CHUNK)
        pltpu.make_async_copy(recvh.at[now], recvh.at[now], h_recv.at[c]).wait()
        left = recvh[now].reshape(CHUNK * blk, width)
        step = 256
        for n in range(rank // step):
            cols = slice(n * step, (n + 1) * step)
            part = dot(left, dt[cols, :], NT).astype(bf16)
            proj[now, :, cols] = part.reshape(CHUNK, blk, step)
        pltpu.make_async_remote_copy(
            proj.at[now], below.at[now], p_send.at[0], below_sem.at[c],
            device_id=(after, me), device_id_type=MESH,
        ).start()
        pltpu.make_async_remote_copy(
            proj.at[now], above.at[now], p_send.at[1], above_sem.at[c],
            device_id=(before, me), device_id_type=MESH,
        ).start()

    def finish(c):
        now = pl.ds(c * CHUNK, CHUNK)
        pltpu.make_async_copy(below.at[now], below.at[now], below_sem.at[c]).wait()
        pltpu.make_async_copy(above.at[now], above.at[now], above_sem.at[c]).wait()
        for i in range(CHUNK):
            mid = proj[c * CHUNK + i].astype(f32)
            hole = (
                columns[0][:, :1] * below[c * CHUNK + i].astype(f32)
                + columns[1][:, :1] * mid
                + columns[2][:, :1] * above[c * CHUNK + i].astype(f32)
            )
            dressed[i * blk : (i + 1) * blk, :] = (
                coupling[...].astype(f32) * mid + hole
            ).astype(bf16)

        @pl.loop(0, SIDE)
        def _(k):
            r = lax.rem(y + k + 1, SIDE)
            cols = pl.ds(pl.multiple_of(r * SIDE * rows, SIDE * rows), SIDE * rows)
            part = dot(dressed[...], dt[:, cols], NN).astype(bf16)
            bbuf[now, :, cols] = part.reshape(CHUNK, blk, SIDE * rows)
            for w in range(SIDE):
                d = r * SIDE + lax.rem(x + w, SIDE)
                src = bbuf.at[now, :, pl.ds(pl.multiple_of(d * rows, rows), rows)]
                send(src, recvb.at[now, own, :], b_send, b_recv.at[c], d)

    @pl.loop(0, chunks + 1)
    def _(c):
        @pl.when(c < chunks)
        def _():
            project(c)

        @pl.when(c > 0)
        def _():
            finish(c - 1)

    @pl.loop(0, chunks)
    def _(c):
        now = pl.ds(c * CHUNK, CHUNK)
        pltpu.make_async_copy(recvb.at[now], recvb.at[now], b_recv.at[c]).wait()

        @pl.when(c < chunks - 1)
        def _():
            left = ladder_left(recvb, c)
            for cols in ladder_steps(width):
                ladder_part(left, c, cols, dt, amp, col, row, occ_i, ladder, c)

    def sent(ref, sem):
        pltpu.make_async_copy(ref, ref, sem).wait()

    sent(pack.at[:, pl.ds(0, (PLANE - 1) * keep), :], pack_sem)
    sent(all_slots.at[pl.ds(0, pairs - 1)], slot_send)
    units = (SIDE - 1) * (2 + 2 * SIDE) * two_here
    sent(full.at[pl.ds(0, units // 2)], full_send)
    sent(ready.at[pl.ds(0, pairs - 1)], share_out)
    sent(hbuf.at[:, pl.ds(blk, (PLANE - 1) * blk), :], h_send)
    sent(proj, p_send.at[0])
    sent(proj, p_send.at[1])
    sent(bbuf.at[:, :, pl.ds(rows, (PLANE - 1) * rows)], b_send)
    for kind, offsets in (("a1", (0,)), ("a2", (0,)), ("b1", (0, 1, -1, 2)), ("b2", (0, 1, -1, 2))):
        each(kind, offsets, lambda m: m.wait_send())


def on_device(amplitudes, factor, home, domains, coupling, hole_weight, virt_energy, occ_i, occ_j):
    pairs = lax.axis_size("pair")
    ni, rows, width = amplitudes.shape[1:]
    stored, rank = factor.shape
    tiles_here = stored // TILE
    tiles = home.shape[0]
    blk = rank // PLANE
    lines = virt_energy.shape[0] // (2 * TILE)

    f32, bf16, i32 = jnp.float32, jnp.bfloat16, jnp.int32
    dma = pltpu.SemaphoreType.DMA
    chunks = ni // CHUNK
    done = ni - CHUNK
    vmem = pl.BlockSpec(memory_space=pltpu.VMEM)
    smem = pl.BlockSpec(memory_space=pltpu.SMEM)
    hbm = pl.BlockSpec(memory_space=pltpu.HBM)
    held = pl.pallas_call(
        residual_kernel,
        out_shape=(
            pltpu.VMEM((done, rows, width), f32),
            pltpu.VMEM((ni * rows, width), bf16),
            pltpu.VMEM((rank, width), bf16),
            pltpu.VMEM((ni, rank, rows), bf16),
            pltpu.VMEM((1, width), f32),
            pltpu.VMEM((rows, rows), f32),
        ),
        in_specs=[hbm] * 8 + [smem],
        out_specs=(vmem,) * 6,
        scratch_shapes=[
            pltpu.VMEM((tiles_here, TILE, rank), bf16),
            pltpu.VMEM((1, tiles), i32),
            pltpu.VMEM(domains.shape, i32),
            pltpu.VMEM((blk, rank), bf16),
            pltpu.VMEM((3, blk), bf16),
            pltpu.VMEM((lines, 2 * TILE), f32),
            pltpu.SMEM((ni,), f32),
            pltpu.VMEM((8, 128), i32),
            pltpu.SMEM((8, 128), i32),
            pltpu.VMEM((3, blk, 128), f32),
            pltpu.VMEM((pairs, 1, 128), i32),
            pltpu.SMEM((pairs, 1, 128), i32),
            pltpu.VMEM((tiles, PLANE * SHARE // pairs, 2 * TILE), bf16),
            pltpu.VMEM((pairs, PLANE * SHARE // pairs, width), bf16),
            pltpu.VMEM((CAP // 2, rank, 2 * TILE), bf16),
            pltpu.VMEM((PLANE * CAP // 2, blk - SHARE, 2 * TILE), bf16),
            pltpu.VMEM((ni, rank, rows), bf16),
            pltpu.VMEM((ni, blk, width), bf16),
            pltpu.VMEM((ni, blk, rank), bf16),
            pltpu.VMEM((ni, blk, rank), bf16),
            pltpu.VMEM((ni, blk, rank), bf16),
            pltpu.VMEM((CHUNK * blk, rank), bf16),
            pltpu.VMEM((ni, blk, width), bf16),
            dma((8,)),
            dma,
            dma,
            dma,
            dma((4,)),
            dma,
            dma,
            dma,
            dma((2,)),
            dma((40,)),
            dma((40,)),
            dma,
            dma((chunks,)),
            dma((2,)),
            dma((chunks,)),
            dma((chunks,)),
            dma,
            dma((chunks,)),
        ],
        compiler_params=pltpu.CompilerParams(
            collective_id=0, has_side_effects=True, vmem_limit_bytes=40 * 2**20
        ),
    )(
        factor.reshape(tiles_here, TILE, rank),
        home[None, :],
        domains,
        amplitudes.reshape(ni * rows, width),
        coupling,
        hole_weight[0],
        virt_energy.reshape(lines, 2 * TILE),
        occ_i,
        occ_j,
    )
    residual = pl.pallas_call(
        last_kernel,
        out_shape=jax.ShapeDtypeStruct((ni, rows, width), f32),
        in_specs=[smem] + [vmem] * 6,
        out_specs=hbm,
        scratch_shapes=[
            pltpu.VMEM((CHUNK, rows, width), f32),
            dma((done,)),
            dma((len(ladder_steps(width)),)),
        ],
        compiler_params=pltpu.CompilerParams(vmem_limit_bytes=16 * 2**20),
    )(occ_i, *held)
    return residual[None]


def solution(mesh):
    placed = (
        P("pair", None, "virt", None),
        P("virt", None),
        P(),
        P("pair", None),
        P("virt", None),
        P("pair", None, "virt"),
        P(),
        P(),
        P("pair"),
    )
    return jax.shard_map(
        on_device,
        mesh=mesh,
        in_specs=placed,
        out_specs=P("pair", None, "virt", None),
        check_vma=False,
    )
```

```python
import jax
import jax.numpy as jnp
from jax import lax
from jax.experimental import pallas as pl
from jax.experimental.pallas import tpu as pltpu
from jax.sharding import PartitionSpec as P

TILE = 64
CAP = 4
SIDE = 4
PLANE = SIDE * SIDE
CHUNK = 2
SHARE = 16
MESH = pl.DeviceIdType.MESH
NT = (((1,), (1,)), ((), ()))
NN = (((1,), (0,)), ((), ()))


def dot(a, b, dims):
    return lax.dot_general(a, b, dims, preferred_element_type=jnp.float32)


def ladder_steps(width):
    return [slice(b, b + 512) for b in range(0, width, 512)]


def ladder_left(recvb, c):
    return jnp.concatenate([recvb[c * CHUNK + i].T for i in range(CHUNK)], axis=0)


def ladder_part(left, c, cols, dt, amp, col, row, occ_i, out, slot):
    rows = left.shape[0] // CHUNK
    part = dot(left, dt[:, cols], NN)
    for i in range(CHUNK):
        lines = pl.ds(pl.multiple_of((c * CHUNK + i) * rows, rows), rows)
        shift = row[:, :1] + (col[:, cols] - occ_i[c * CHUNK + i])
        out[slot * CHUNK + i, :, cols] = part[i * rows : (i + 1) * rows] + shift * amp[
            lines, cols
        ].astype(jnp.float32)


def last_kernel(occ_i, ladder, amp, dt, recvb, col, row, out_hbm, last, sem, last_sem):
    done = ladder.shape[0]
    c = done // CHUNK
    copies = [pltpu.make_async_copy(ladder.at[i], out_hbm.at[i], sem.at[i]) for i in range(done)]
    for copy in copies:
        copy.start()
    left = ladder_left(recvb, c)
    for k, cols in enumerate(ladder_steps(dt.shape[1])):
        ladder_part(left, c, cols, dt, amp, col, row, occ_i, last, 0)
        copy = pltpu.make_async_copy(
            last.at[:, :, cols], out_hbm.at[pl.ds(done, CHUNK), :, cols], last_sem.at[k]
        )
        copy.start()
        copies.append(copy)
    for copy in copies:
        copy.wait()


def residual_kernel(
    factor_hbm,
    home_hbm,
    domain_hbm,
    amp_hbm,
    coupling_hbm,
    weight_hbm,
    energy_hbm,
    occ_i_hbm,
    occ_j,
    ladder,
    amp,
    dt,
    recvb,
    col,
    row,
    factor,
    home,
    domain,
    coupling,
    weight,
    energy,
    occ_i,
    table,
    where,
    columns,
    all_slots,
    slot_lists,
    full,
    ready,
    pack,
    got_up,
    hbuf,
    recvh,
    proj,
    below,
    above,
    dressed,
    bbuf,
    io_sem,
    slot_send,
    slot_recv,
    full_send,
    full_recv,
    share_out,
    share_in,
    pack_sem,
    got_sem,
    ag_send,
    ag_recv,
    h_send,
    h_recv,
    p_send,
    below_sem,
    above_sem,
    b_send,
    b_recv,
):
    f32, bf16, i32 = jnp.float32, jnp.bfloat16, jnp.int32
    pairs = lax.axis_size("pair")
    pair = lax.axis_index("pair")
    me = lax.axis_index("virt")
    y, x = lax.div(me, SIDE), lax.rem(me, SIDE)
    after = lax.rem(pair + 1, pairs)
    before = lax.rem(pair + pairs - 1, pairs)
    rank, width = dt.shape
    blk = rank // PLANE
    rows = width // PLANE
    chunks = hbuf.shape[0] // CHUNK
    tiles_here = factor.shape[0]
    in_domain = width // TILE

    barrier = pltpu.get_barrier_semaphore()

    @pl.loop(1, PLANE)
    def _(s):
        pl.semaphore_signal(
            barrier, inc=1, device_id=(pair, lax.rem(me + s, PLANE)), device_id_type=MESH
        )

    @pl.loop(1, pairs)
    def _(s):
        pl.semaphore_signal(
            barrier, inc=1, device_id=(lax.rem(pair + s, pairs), me), device_id_type=MESH
        )

    def fetch(k, src, dst):
        copy = pltpu.make_async_copy(src, dst, io_sem.at[k])
        copy.start()
        return copy

    get_home = fetch(0, home_hbm, home)
    get_domain = fetch(1, domain_hbm, domain)
    get_factor = fetch(2, factor_hbm, factor)
    get_small = [
        fetch(3, coupling_hbm, coupling),
        fetch(4, weight_hbm, weight),
        fetch(5, energy_hbm, energy),
        fetch(6, occ_i_hbm, occ_i),
    ]
    get_amp = fetch(7, amp_hbm, amp)

    get_home.wait()
    get_domain.wait()
    tiles = home.shape[1]
    home_row = jnp.broadcast_to(home[...], (in_domain, tiles))
    domain_row = jnp.broadcast_to(domain[...], (tiles, in_domain))
    slots = lax.broadcasted_iota(i32, (in_domain, tiles), 1)
    slot_col = jnp.max(jnp.where(home_row == domain_row.T, slots, 0), axis=1, keepdims=True)
    slots = lax.broadcasted_iota(i32, (tiles, in_domain), 0)
    slot_row = jnp.max(jnp.where(home_row.T == domain_row, slots, 0), axis=0, keepdims=True)
    holder_col, holder_row = lax.div(slot_col, tiles_here), lax.div(slot_row, tiles_here)
    same = holder_col == holder_row
    up = lax.broadcasted_iota(i32, (in_domain, in_domain), 0)
    across = lax.broadcasted_iota(i32, (in_domain, in_domain), 1)
    nth_row = jnp.sum(jnp.where(same & (up < across), 1, 0), axis=0, keepdims=True)
    nth_col = jnp.sum(jnp.where(same & (across < up), 1, 0), axis=1, keepdims=True)
    nth_row, nth_col = jnp.minimum(nth_row, CAP - 1), jnp.minimum(nth_col, CAP - 1)
    number = lax.broadcasted_iota(i32, (in_domain, 128), 1)
    mine = jnp.max(
        jnp.where(
            (holder_col == me) & (nth_col == number), lax.rem(slot_col, tiles_here), 0
        ),
        axis=0,
        keepdims=True,
    )
    table[0:1, 0:in_domain] = holder_row * (CAP // 2) + lax.div(nth_row, 2)
    table[1:2, 0:in_domain] = lax.rem(nth_row, 2)
    table[2:3, 0:in_domain] = lax.div(domain[...], 2)
    table[3:4, 0:in_domain] = lax.rem(domain[...], 2)
    table[4:5, :] = mine
    table[5:8, :] = jnp.zeros((3, 128), i32)
    scalars = fetch(0, table, where)
    all_slots[pair] = jnp.zeros((1, 128), i32)
    turn = lax.rem(slot_row + lax.broadcasted_iota(i32, (1, in_domain), 1), 2)
    all_slots[pair, :, 0:in_domain] = lax.div(slot_row, 2) + turn * (tiles // 2)
    scalars.wait()

    get_factor.wait()
    for c in range(CAP // 2):
        two = jnp.concatenate([factor[where[4, 2 * c]], factor[where[4, 2 * c + 1]]], axis=0)
        pack[c] = two.T

    keep = blk - SHARE
    per = PLANE // pairs
    rank_cols = pl.ds(pl.multiple_of(pair * per * blk, per * blk), per * blk)
    wide = factor[:, :, rank_cols].reshape(tiles_here * TILE, per * blk).T
    wide = jnp.concatenate([wide[k * blk + keep : (k + 1) * blk] for k in range(per)], axis=0)
    two_here = tiles_here // 2
    for k in range(two_here):
        full[me * two_here + k] = wide[:, k * 2 * TILE : (k + 1) * 2 * TILE]

    pl.semaphore_wait(barrier, PLANE + pairs - 2)

    hs = per * SHARE // 2

    @pl.loop(1, pairs)
    def _(s):
        pltpu.make_async_remote_copy(
            all_slots.at[pair], all_slots.at[pair], slot_send, slot_recv,
            device_id=(lax.rem(pair + s, pairs), me), device_id_type=MESH,
        ).start()

    def share_send(first, n, h, sem, to):
        part = full.at[pl.ds(first, n), h * hs : (h + 1) * hs, :]
        pltpu.make_async_remote_copy(
            part, part, full_send, full_recv.at[sem], device_id=(pair, to), device_id_type=MESH
        ).start()

    def to_x(s):
        return y * SIDE + lax.rem(x + s, SIDE)

    def to_y(s):
        return lax.rem(y + s, SIDE) * SIDE + x

    for s in range(1, SIDE):
        share_send(me * two_here, two_here, 0, 0, to_x(s))
        share_send(me * two_here, two_here, 1, 1, to_y(s))

    got = (got_up,)
    offs = (0,)

    def pack_part(d, h):
        return pack.at[:, pl.ds(pl.multiple_of(d * blk + offs[h], 16), got[h].shape[1]), :]

    for h in range(1):
        here = got[h].at[pl.ds(me * (CAP // 2), CAP // 2)]

        @pl.loop(1, PLANE)
        def _(s):
            d = lax.rem(me + s, PLANE)
            pltpu.make_async_remote_copy(
                pack_part(d, h), here, pack_sem, got_sem.at[h],
                device_id=(pair, d), device_id_type=MESH,
            ).start()

        pltpu.make_async_copy(pack_part(me, h), here, got_sem.at[h]).start()

    def share_landed(n, h, sem):
        part = full.at[pl.ds(0, n), h * hs : (h + 1) * hs, :]
        pltpu.make_async_copy(part, part, full_recv.at[sem]).wait()

    share_landed((SIDE - 1) * two_here, 0, 0)
    for s in range(1, SIDE):
        share_send(y * SIDE * two_here, SIDE * two_here, 0, 2, to_y(s))
    share_landed((SIDE - 1) * two_here, 1, 1)
    for s in range(1, SIDE):
        for k in range(SIDE):
            share_send((k * SIDE + x) * two_here, two_here, 1, 3, to_x(s))

    low = lax.broadcasted_iota(i32, (blk, 2 * TILE), 1) < TILE

    def swapped(wide):
        return jnp.concatenate([wide[:, TILE:], wide[:, :TILE]], axis=1)

    own = pl.ds(pl.multiple_of(me * blk, blk), blk)

    def arrange(h):
        pltpu.make_async_copy(got[h], got[h], got_sem.at[h]).wait()
        lines = pl.ds(pl.multiple_of(me * blk + offs[h], 16), got[h].shape[1])
        for u in range(in_domain // 2):
            even, odd = [
                jnp.where(where[1, t] == t % 2, wide, swapped(wide))
                for t in (2 * u, 2 * u + 1)
                for wide in (got[h][where[0, t]],)
            ]
            dt[lines, u * 2 * TILE : (u + 1) * 2 * TILE] = jnp.where(
                low[: even.shape[0]], even, odd
            )

    def device(dy, dx):
        return lax.rem(y + dy + SIDE, SIDE) * SIDE + lax.rem(x + dx + SIDE, SIDE)

    def at(axis, along, other):
        return device(other, along) if axis == 0 else device(along, other)

    names = {}

    def message(kind, h, s, sign):
        k = names.setdefault((kind, h, s, sign), len(names))
        if kind == "a1":
            block, to = at(h, 0, 0), at(h, sign, 0)
        elif kind == "a2":
            block, to = at(h, -sign, 0), at(h, sign, 0)
        elif kind == "b1":
            block, to = at(h, s, 0), at(h, 0, sign)
        else:
            block, to = at(h, s, -sign), at(h, 0, sign)
        if kind in ("a1", "b1"):
            off, n = h * (width // 2), width // 2
        else:
            off, n = h * (width // 2) + (0 if sign > 0 else width // 4), width // 4
        part = dt.at[pl.ds(pl.multiple_of(block * blk, blk), keep), off : off + n]
        return pltpu.make_async_remote_copy(
            part, part, ag_send.at[k], ag_recv.at[k], device_id=(pair, to), device_id_type=MESH
        )

    def each(kind, offsets, do):
        for s in offsets:
            for h in (0, 1):
                for sign in (1, -1):
                    do(message(kind, h, s, sign))

    def go(m):
        m.start()

    def landed(m):
        m.wait_recv()

    def send(src, dst, send_sem, recv_sem, d):
        @pl.when(d != me)
        def _():
            pltpu.make_async_remote_copy(
                src, dst, send_sem, recv_sem, device_id=(pair, d), device_id_type=MESH
            ).start()

        @pl.when(d == me)
        def _():
            pltpu.make_async_copy(src, dst, recv_sem).start()

    def band_of(d):
        return pl.ds(pl.multiple_of(d * blk, blk), blk)

    def half(c, r):
        now = pl.ds(c * CHUNK, CHUNK)
        band = pl.ds(pl.multiple_of(r * SIDE * blk, SIDE * blk), SIDE * blk)
        lines = pl.ds(pl.multiple_of(c * CHUNK * rows, CHUNK * rows), CHUNK * rows)
        part = dot(dt[band, :], amp[lines, :], NT).astype(bf16)
        for i in range(CHUNK):
            hbuf[c * CHUNK + i, band, :] = part[:, i * rows : (i + 1) * rows]
        for w in range(SIDE):
            d = r * SIDE + lax.rem(x + w, SIDE)
            send(
                hbuf.at[now, band_of(d), :],
                recvh.at[now, :, pl.ds(pl.multiple_of(me * rows, rows), rows)],
                h_send,
                h_recv.at[c],
                d,
            )

    arrange(0)
    each("a1", (0,), go)
    each("b1", (0,), go)

    pltpu.make_async_copy(
        all_slots.at[pl.ds(0, pairs - 1)], all_slots.at[pl.ds(0, pairs - 1)], slot_recv
    ).wait()
    lists = fetch(0, all_slots, slot_lists)
    share_landed((SIDE - 1) * SIDE * two_here, 0, 2)
    share_landed((SIDE - 1) * SIDE * two_here, 1, 3)
    for k in range(tiles // 2):
        full[tiles // 2 + k] = swapped(full[k])
    lists.wait()

    def hand_out(first, last):
        @pl.loop(first, last)
        def _(k):
            p = lax.rem(pair + pairs // 2 + k, pairs)

            for u in range(in_domain // 2):
                ready[p, :, u * 2 * TILE : (u + 1) * 2 * TILE] = jnp.where(
                    low[: full.shape[1]],
                    full[slot_lists[p, 0, 2 * u]],
                    full[slot_lists[p, 0, 2 * u + 1]],
                )

            for b in range(per):
                src = ready.at[p, b * SHARE : (b + 1) * SHARE, :]
                start = pl.multiple_of((pair * per + b) * blk + keep, SHARE)
                dst = dt.at[pl.ds(start, SHARE), :]

                @pl.when(p != pair)
                def _():
                    pltpu.make_async_remote_copy(
                        src, dst, share_out, share_in, device_id=(p, me), device_id_type=MESH
                    ).start()

                @pl.when(p == pair)
                def _():
                    pltpu.make_async_copy(src, dst, share_in).start()

    hand_out(0, 3)
    for h in (0, 1):
        for sign in (1, -1):
            message("a1", h, 0, sign).wait_recv()
            message("a2", h, 0, sign).start()
    each("b1", (1, -1), go)
    hand_out(3, 5)
    each("b1", (0,), landed)
    each("b2", (0,), go)
    each("a2", (0,), landed)
    each("b1", (2,), go)
    hand_out(5, pairs)

    for copy in get_small:
        copy.wait()

    def halves(wide, second):
        return jnp.where(second == 1, wide[:, TILE:], wide[:, :TILE])

    def energy_of(t):
        return halves(energy[pl.ds(where[2, t], 1), :], where[3, t])

    for u in range(in_domain // 2):
        col[:, u * 2 * TILE : (u + 1) * 2 * TILE] = jnp.concatenate(
            [energy_of(2 * u), energy_of(2 * u + 1)], axis=1
        )
    here_energy = col[:, pl.ds(pl.multiple_of(me * rows, rows), rows)]
    row[...] = jnp.broadcast_to(here_energy, (rows, rows)).T - occ_j[0]
    has = (jnp.where(pair > 0, 1.0, 0.0), 1.0, jnp.where(pair < pairs - 1, 1.0, 0.0))
    for d in range(3):
        line = weight[d : d + 1, :].astype(f32) * has[d]
        columns[d] = jnp.broadcast_to(line, (128, blk)).T

    each("b2", (0,), landed)
    each("b1", (1, -1), landed)
    each("b2", (1, -1), go)
    each("b1", (2,), landed)
    each("b2", (2,), go)

    each("b2", (1, -1, 2), landed)
    all_shares = dt.at[pl.ds(0, PLANE * SHARE), :]
    pltpu.make_async_copy(all_shares, all_shares, share_in).wait()
    get_amp.wait()

    @pl.loop(0, chunks)
    def _(c):
        @pl.loop(0, SIDE)
        def _(k):
            half(c, lax.rem(y + k + 1, SIDE))

    def project(c):
        now = pl.ds(c * CHUNK, CHUNK)
        pltpu.make_async_copy(recvh.at[now], recvh.at[now], h_recv.at[c]).wait()
        left = recvh[now].reshape(CHUNK * blk, width)
        step = 256
        for n in range(rank // step):
            cols = slice(n * step, (n + 1) * step)
            part = dot(left, dt[cols, :], NT).astype(bf16)
            proj[now, :, cols] = part.reshape(CHUNK, blk, step)
        pltpu.make_async_remote_copy(
            proj.at[now], below.at[now], p_send.at[0], below_sem.at[c],
            device_id=(after, me), device_id_type=MESH,
        ).start()
        pltpu.make_async_remote_copy(
            proj.at[now], above.at[now], p_send.at[1], above_sem.at[c],
            device_id=(before, me), device_id_type=MESH,
        ).start()

    def finish(c):
        now = pl.ds(c * CHUNK, CHUNK)
        pltpu.make_async_copy(below.at[now], below.at[now], below_sem.at[c]).wait()
        pltpu.make_async_copy(above.at[now], above.at[now], above_sem.at[c]).wait()
        for i in range(CHUNK):
            mid = proj[c * CHUNK + i].astype(f32)
            hole = (
                columns[0][:, :1] * below[c * CHUNK + i].astype(f32)
                + columns[1][:, :1] * mid
                + columns[2][:, :1] * above[c * CHUNK + i].astype(f32)
            )
            dressed[i * blk : (i + 1) * blk, :] = (
                coupling[...].astype(f32) * mid + hole
            ).astype(bf16)

        @pl.loop(0, SIDE)
        def _(k):
            r = lax.rem(y + k + 1, SIDE)
            cols = pl.ds(pl.multiple_of(r * SIDE * rows, SIDE * rows), SIDE * rows)
            part = dot(dressed[...], dt[:, cols], NN).astype(bf16)
            bbuf[now, :, cols] = part.reshape(CHUNK, blk, SIDE * rows)
            for w in range(SIDE):
                d = r * SIDE + lax.rem(x + w, SIDE)
                src = bbuf.at[now, :, pl.ds(pl.multiple_of(d * rows, rows), rows)]
                send(src, recvb.at[now, own, :], b_send, b_recv.at[c], d)

    @pl.loop(0, chunks + 1)
    def _(c):
        @pl.when(c < chunks)
        def _():
            project(c)

        @pl.when(c > 0)
        def _():
            finish(c - 1)

    @pl.loop(0, chunks)
    def _(c):
        now = pl.ds(c * CHUNK, CHUNK)
        pltpu.make_async_copy(recvb.at[now], recvb.at[now], b_recv.at[c]).wait()

        @pl.when(c < chunks - 1)
        def _():
            left = ladder_left(recvb, c)
            for cols in ladder_steps(width):
                ladder_part(left, c, cols, dt, amp, col, row, occ_i, ladder, c)

    def sent(ref, sem):
        pltpu.make_async_copy(ref, ref, sem).wait()

    sent(pack.at[:, pl.ds(0, (PLANE - 1) * keep), :], pack_sem)
    sent(all_slots.at[pl.ds(0, pairs - 1)], slot_send)
    units = (SIDE - 1) * (2 + 2 * SIDE) * two_here
    sent(full.at[pl.ds(0, units // 2)], full_send)
    sent(ready.at[pl.ds(0, pairs - 1)], share_out)
    sent(hbuf.at[:, pl.ds(blk, (PLANE - 1) * blk), :], h_send)
    sent(proj, p_send.at[0])
    sent(proj, p_send.at[1])
    sent(bbuf.at[:, :, pl.ds(rows, (PLANE - 1) * rows)], b_send)
    for kind, offsets in (("a1", (0,)), ("a2", (0,)), ("b1", (0, 1, -1, 2)), ("b2", (0, 1, -1, 2))):
        each(kind, offsets, lambda m: m.wait_send())


def on_device(amplitudes, factor, home, domains, coupling, hole_weight, virt_energy, occ_i, occ_j):
    pairs = lax.axis_size("pair")
    ni, rows, width = amplitudes.shape[1:]
    stored, rank = factor.shape
    tiles_here = stored // TILE
    tiles = home.shape[0]
    blk = rank // PLANE
    lines = virt_energy.shape[0] // (2 * TILE)

    f32, bf16, i32 = jnp.float32, jnp.bfloat16, jnp.int32
    dma = pltpu.SemaphoreType.DMA
    chunks = ni // CHUNK
    done = ni - CHUNK
    vmem = pl.BlockSpec(memory_space=pltpu.VMEM)
    smem = pl.BlockSpec(memory_space=pltpu.SMEM)
    hbm = pl.BlockSpec(memory_space=pltpu.HBM)
    held = pl.pallas_call(
        residual_kernel,
        out_shape=(
            pltpu.VMEM((done, rows, width), f32),
            pltpu.VMEM((ni * rows, width), bf16),
            pltpu.VMEM((rank, width), bf16),
            pltpu.VMEM((ni, rank, rows), bf16),
            pltpu.VMEM((1, width), f32),
            pltpu.VMEM((rows, rows), f32),
        ),
        in_specs=[hbm] * 8 + [smem],
        out_specs=(vmem,) * 6,
        scratch_shapes=[
            pltpu.VMEM((tiles_here, TILE, rank), bf16),
            pltpu.VMEM((1, tiles), i32),
            pltpu.VMEM(domains.shape, i32),
            pltpu.VMEM((blk, rank), bf16),
            pltpu.VMEM((3, blk), bf16),
            pltpu.VMEM((lines, 2 * TILE), f32),
            pltpu.SMEM((ni,), f32),
            pltpu.VMEM((8, 128), i32),
            pltpu.SMEM((8, 128), i32),
            pltpu.VMEM((3, blk, 128), f32),
            pltpu.VMEM((pairs, 1, 128), i32),
            pltpu.SMEM((pairs, 1, 128), i32),
            pltpu.VMEM((tiles, PLANE * SHARE // pairs, 2 * TILE), bf16),
            pltpu.VMEM((pairs, PLANE * SHARE // pairs, width), bf16),
            pltpu.VMEM((CAP // 2, rank, 2 * TILE), bf16),
            pltpu.VMEM((PLANE * CAP // 2, blk - SHARE, 2 * TILE), bf16),
            pltpu.VMEM((ni, rank, rows), bf16),
            pltpu.VMEM((ni, blk, width), bf16),
            pltpu.VMEM((ni, blk, rank), bf16),
            pltpu.VMEM((ni, blk, rank), bf16),
            pltpu.VMEM((ni, blk, rank), bf16),
            pltpu.VMEM((CHUNK * blk, rank), bf16),
            pltpu.VMEM((ni, blk, width), bf16),
            dma((8,)),
            dma,
            dma,
            dma,
            dma((4,)),
            dma,
            dma,
            dma,
            dma((2,)),
            dma((40,)),
            dma((40,)),
            dma,
            dma((chunks,)),
            dma((2,)),
            dma((chunks,)),
            dma((chunks,)),
            dma,
            dma((chunks,)),
        ],
        compiler_params=pltpu.CompilerParams(
            collective_id=0, has_side_effects=True, vmem_limit_bytes=40 * 2**20
        ),
    )(
        factor.reshape(tiles_here, TILE, rank),
        home[None, :],
        domains,
        amplitudes.reshape(ni * rows, width),
        coupling,
        hole_weight[0],
        virt_energy.reshape(lines, 2 * TILE),
        occ_i,
        occ_j,
    )
    residual = pl.pallas_call(
        last_kernel,
        out_shape=jax.ShapeDtypeStruct((ni, rows, width), f32),
        in_specs=[smem] + [vmem] * 6,
        out_specs=hbm,
        scratch_shapes=[
            pltpu.VMEM((CHUNK, rows, width), f32),
            dma((done,)),
            dma((len(ladder_steps(width)),)),
        ],
        compiler_params=pltpu.CompilerParams(vmem_limit_bytes=16 * 2**20),
    )(occ_i, *held)
    return residual[None]


def solution(mesh):
    placed = (
        P("pair", None, "virt", None),
        P("virt", None),
        P(),
        P("pair", None),
        P("virt", None),
        P("pair", None, "virt"),
        P(),
        P(),
        P("pair"),
    )
    return jax.shard_map(
        on_device,
        mesh=mesh,
        in_specs=placed,
        out_specs=P("pair", None, "virt", None),
        check_vma=False,
    )
```

```python
import jax
import jax.numpy as jnp
from jax import lax
from jax.experimental import pallas as pl
from jax.experimental.pallas import tpu as pltpu
from jax.sharding import PartitionSpec as P

TILE = 64
CAP = 4
SIDE = 4
PLANE = SIDE * SIDE
CHUNK = 2
SHARE = 16
MESH = pl.DeviceIdType.MESH
NT = (((1,), (1,)), ((), ()))
NN = (((1,), (0,)), ((), ()))


def dot(a, b, dims):
    return lax.dot_general(a, b, dims, preferred_element_type=jnp.float32)


def ladder_steps(width):
    return [slice(b, b + 512) for b in range(0, width, 512)]


def ladder_left(recvb, c):
    return jnp.concatenate([recvb[c * CHUNK + i].T for i in range(CHUNK)], axis=0)


def ladder_part(left, c, cols, dt, amp, col, row, occ_i, out, slot):
    rows = left.shape[0] // CHUNK
    part = dot(left, dt[:, cols], NN)
    for i in range(CHUNK):
        lines = pl.ds(pl.multiple_of((c * CHUNK + i) * rows, rows), rows)
        shift = row[:, :1] + (col[:, cols] - occ_i[c * CHUNK + i])
        out[slot * CHUNK + i, :, cols] = part[i * rows : (i + 1) * rows] + shift * amp[
            lines, cols
        ].astype(jnp.float32)


def last_kernel(occ_i, ladder, amp, dt, recvb, col, row, out_hbm, last, sem, last_sem):
    done = ladder.shape[0]
    c = done // CHUNK
    copies = [pltpu.make_async_copy(ladder, out_hbm.at[pl.ds(0, done)], sem.at[0])]
    for copy in copies:
        copy.start()
    left = ladder_left(recvb, c)
    for k, cols in enumerate(ladder_steps(dt.shape[1])):
        ladder_part(left, c, cols, dt, amp, col, row, occ_i, last, 0)
        copy = pltpu.make_async_copy(
            last.at[:, :, cols], out_hbm.at[pl.ds(done, CHUNK), :, cols], last_sem.at[k]
        )
        copy.start()
        copies.append(copy)
    for copy in copies:
        copy.wait()


def residual_kernel(
    factor_hbm,
    home_hbm,
    domain_hbm,
    amp_hbm,
    coupling_hbm,
    weight_hbm,
    energy_hbm,
    occ_i_hbm,
    occ_j,
    ladder,
    amp,
    dt,
    recvb,
    col,
    row,
    factor,
    home,
    domain,
    coupling,
    weight,
    energy,
    occ_i,
    table,
    where,
    columns,
    all_slots,
    slot_lists,
    full,
    ready,
    pack,
    got_up,
    hbuf,
    recvh,
    proj,
    below,
    above,
    dressed,
    bbuf,
    io_sem,
    slot_send,
    slot_recv,
    full_send,
    full_recv,
    share_out,
    share_in,
    pack_sem,
    got_sem,
    ag_send,
    ag_recv,
    h_send,
    h_recv,
    p_send,
    below_sem,
    above_sem,
    b_send,
    b_recv,
):
    f32, bf16, i32 = jnp.float32, jnp.bfloat16, jnp.int32
    pairs = lax.axis_size("pair")
    pair = lax.axis_index("pair")
    me = lax.axis_index("virt")
    y, x = lax.div(me, SIDE), lax.rem(me, SIDE)
    after = lax.rem(pair + 1, pairs)
    before = lax.rem(pair + pairs - 1, pairs)
    rank, width = dt.shape
    blk = rank // PLANE
    rows = width // PLANE
    chunks = hbuf.shape[0] // CHUNK
    tiles_here = factor.shape[0]
    in_domain = width // TILE

    barrier = pltpu.get_barrier_semaphore()

    @pl.loop(1, PLANE)
    def _(s):
        pl.semaphore_signal(
            barrier, inc=1, device_id=(pair, lax.rem(me + s, PLANE)), device_id_type=MESH
        )

    @pl.loop(1, pairs)
    def _(s):
        pl.semaphore_signal(
            barrier, inc=1, device_id=(lax.rem(pair + s, pairs), me), device_id_type=MESH
        )

    def fetch(k, src, dst):
        copy = pltpu.make_async_copy(src, dst, io_sem.at[k])
        copy.start()
        return copy

    get_home = fetch(0, home_hbm, home)
    get_domain = fetch(1, domain_hbm, domain)
    get_factor = fetch(2, factor_hbm, factor)
    get_small = [
        fetch(3, coupling_hbm, coupling),
        fetch(4, weight_hbm, weight),
        fetch(5, energy_hbm, energy),
        fetch(6, occ_i_hbm, occ_i),
    ]
    get_amp = fetch(7, amp_hbm, amp)

    get_home.wait()
    get_domain.wait()
    tiles = home.shape[1]
    home_row = jnp.broadcast_to(home[...], (in_domain, tiles))
    domain_row = jnp.broadcast_to(domain[...], (tiles, in_domain))
    slots = lax.broadcasted_iota(i32, (in_domain, tiles), 1)
    slot_col = jnp.max(jnp.where(home_row == domain_row.T, slots, 0), axis=1, keepdims=True)
    slots = lax.broadcasted_iota(i32, (tiles, in_domain), 0)
    slot_row = jnp.max(jnp.where(home_row.T == domain_row, slots, 0), axis=0, keepdims=True)
    holder_col, holder_row = lax.div(slot_col, tiles_here), lax.div(slot_row, tiles_here)
    same = holder_col == holder_row
    up = lax.broadcasted_iota(i32, (in_domain, in_domain), 0)
    across = lax.broadcasted_iota(i32, (in_domain, in_domain), 1)
    nth_row = jnp.sum(jnp.where(same & (up < across), 1, 0), axis=0, keepdims=True)
    nth_col = jnp.sum(jnp.where(same & (across < up), 1, 0), axis=1, keepdims=True)
    nth_row, nth_col = jnp.minimum(nth_row, CAP - 1), jnp.minimum(nth_col, CAP - 1)
    number = lax.broadcasted_iota(i32, (in_domain, 128), 1)
    mine = jnp.max(
        jnp.where(
            (holder_col == me) & (nth_col == number), lax.rem(slot_col, tiles_here), 0
        ),
        axis=0,
        keepdims=True,
    )
    table[0:1, 0:in_domain] = holder_row * (CAP // 2) + lax.div(nth_row, 2)
    table[1:2, 0:in_domain] = lax.rem(nth_row, 2)
    table[2:3, 0:in_domain] = lax.div(domain[...], 2)
    table[3:4, 0:in_domain] = lax.rem(domain[...], 2)
    table[4:5, :] = mine
    table[5:8, :] = jnp.zeros((3, 128), i32)
    scalars = fetch(0, table, where)
    all_slots[pair] = jnp.zeros((1, 128), i32)
    turn = lax.rem(slot_row + lax.broadcasted_iota(i32, (1, in_domain), 1), 2)
    all_slots[pair, :, 0:in_domain] = lax.div(slot_row, 2) + turn * (tiles // 2)
    scalars.wait()

    get_factor.wait()
    for c in range(CAP // 2):
        two = jnp.concatenate([factor[where[4, 2 * c]], factor[where[4, 2 * c + 1]]], axis=0)
        pack[c] = two.T

    keep = blk - SHARE
    per = PLANE // pairs
    rank_cols = pl.ds(pl.multiple_of(pair * per * blk, per * blk), per * blk)
    wide = factor[:, :, rank_cols].reshape(tiles_here * TILE, per * blk).T
    wide = jnp.concatenate([wide[k * blk + keep : (k + 1) * blk] for k in range(per)], axis=0)
    two_here = tiles_here // 2
    for k in range(two_here):
        full[me * two_here + k] = wide[:, k * 2 * TILE : (k + 1) * 2 * TILE]

    pl.semaphore_wait(barrier, PLANE + pairs - 2)

    hs = per * SHARE // 2

    @pl.loop(1, pairs)
    def _(s):
        pltpu.make_async_remote_copy(
            all_slots.at[pair], all_slots.at[pair], slot_send, slot_recv,
            device_id=(lax.rem(pair + s, pairs), me), device_id_type=MESH,
        ).start()

    def share_send(first, n, h, sem, to):
        part = full.at[pl.ds(first, n), h * hs : (h + 1) * hs, :]
        pltpu.make_async_remote_copy(
            part, part, full_send, full_recv.at[sem], device_id=(pair, to), device_id_type=MESH
        ).start()

    def to_x(s):
        return y * SIDE + lax.rem(x + s, SIDE)

    def to_y(s):
        return lax.rem(y + s, SIDE) * SIDE + x

    for s in range(1, SIDE):
        share_send(me * two_here, two_here, 0, 0, to_x(s))
        share_send(me * two_here, two_here, 1, 1, to_y(s))

    got = (got_up,)
    offs = (0,)

    def pack_part(d, h):
        return pack.at[:, pl.ds(pl.multiple_of(d * blk + offs[h], 16), got[h].shape[1]), :]

    for h in range(1):
        here = got[h].at[pl.ds(me * (CAP // 2), CAP // 2)]

        @pl.loop(1, PLANE)
        def _(s):
            d = lax.rem(me + s, PLANE)
            pltpu.make_async_remote_copy(
                pack_part(d, h), here, pack_sem, got_sem.at[h],
                device_id=(pair, d), device_id_type=MESH,
            ).start()

        pltpu.make_async_copy(pack_part(me, h), here, got_sem.at[h]).start()

    def share_landed(n, h, sem):
        part = full.at[pl.ds(0, n), h * hs : (h + 1) * hs, :]
        pltpu.make_async_copy(part, part, full_recv.at[sem]).wait()

    share_landed((SIDE - 1) * two_here, 0, 0)
    for s in range(1, SIDE):
        share_send(y * SIDE * two_here, SIDE * two_here, 0, 2, to_y(s))
    share_landed((SIDE - 1) * two_here, 1, 1)
    for s in range(1, SIDE):
        for k in range(SIDE):
            share_send((k * SIDE + x) * two_here, two_here, 1, 3, to_x(s))

    for copy in get_small:
        copy.wait()

    def halves(wide, second):
        return jnp.where(second == 1, wide[:, TILE:], wide[:, :TILE])

    low = lax.broadcasted_iota(i32, (blk, 2 * TILE), 1) < TILE

    def swapped(wide):
        return jnp.concatenate([wide[:, TILE:], wide[:, :TILE]], axis=1)

    def energy_of(t):
        return halves(energy[pl.ds(where[2, t], 1), :], where[3, t])

    for u in range(in_domain // 2):
        col[:, u * 2 * TILE : (u + 1) * 2 * TILE] = jnp.concatenate(
            [energy_of(2 * u), energy_of(2 * u + 1)], axis=1
        )
    here_energy = col[:, pl.ds(pl.multiple_of(me * rows, rows), rows)]
    row[...] = jnp.broadcast_to(here_energy, (rows, rows)).T - occ_j[0]
    has = (jnp.where(pair > 0, 1.0, 0.0), 1.0, jnp.where(pair < pairs - 1, 1.0, 0.0))
    for d in range(3):
        line = weight[d : d + 1, :].astype(f32) * has[d]
        columns[d] = jnp.broadcast_to(line, (128, blk)).T

    own = pl.ds(pl.multiple_of(me * blk, blk), blk)

    def arrange(h):
        pltpu.make_async_copy(got[h], got[h], got_sem.at[h]).wait()
        lines = pl.ds(pl.multiple_of(me * blk + offs[h], 16), got[h].shape[1])
        for u in range(in_domain // 2):
            even, odd = [
                jnp.where(where[1, t] == t % 2, wide, swapped(wide))
                for t in (2 * u, 2 * u + 1)
                for wide in (got[h][where[0, t]],)
            ]
            dt[lines, u * 2 * TILE : (u + 1) * 2 * TILE] = jnp.where(
                low[: even.shape[0]], even, odd
            )

    def device(dy, dx):
        return lax.rem(y + dy + SIDE, SIDE) * SIDE + lax.rem(x + dx + SIDE, SIDE)

    def at(axis, along, other):
        return device(other, along) if axis == 0 else device(along, other)

    names = {}

    def message(kind, h, s, sign):
        k = names.setdefault((kind, h, s, sign), len(names))
        if kind == "a1":
            block, to = at(h, 0, 0), at(h, sign, 0)
        elif kind == "a2":
            block, to = at(h, -sign, 0), at(h, sign, 0)
        elif kind == "b1":
            block, to = at(h, s, 0), at(h, 0, sign)
        else:
            block, to = at(h, s, -sign), at(h, 0, sign)
        if kind in ("a1", "b1"):
            off, n = h * (width // 2), width // 2
        else:
            off, n = h * (width // 2) + (0 if sign > 0 else width // 4), width // 4
        part = dt.at[pl.ds(pl.multiple_of(block * blk, blk), keep), off : off + n]
        return pltpu.make_async_remote_copy(
            part, part, ag_send.at[k], ag_recv.at[k], device_id=(pair, to), device_id_type=MESH
        )

    def each(kind, offsets, do):
        for s in offsets:
            for h in (0, 1):
                for sign in (1, -1):
                    do(message(kind, h, s, sign))

    def go(m):
        m.start()

    def landed(m):
        m.wait_recv()

    def send(src, dst, send_sem, recv_sem, d):
        @pl.when(d != me)
        def _():
            pltpu.make_async_remote_copy(
                src, dst, send_sem, recv_sem, device_id=(pair, d), device_id_type=MESH
            ).start()

        @pl.when(d == me)
        def _():
            pltpu.make_async_copy(src, dst, recv_sem).start()

    def band_of(d):
        return pl.ds(pl.multiple_of(d * blk, blk), blk)

    def half(c, r):
        now = pl.ds(c * CHUNK, CHUNK)
        band = pl.ds(pl.multiple_of(r * SIDE * blk, SIDE * blk), SIDE * blk)
        lines = pl.ds(pl.multiple_of(c * CHUNK * rows, CHUNK * rows), CHUNK * rows)
        part = dot(dt[band, :], amp[lines, :], NT).astype(bf16)
        for i in range(CHUNK):
            hbuf[c * CHUNK + i, band, :] = part[:, i * rows : (i + 1) * rows]
        for w in range(SIDE):
            d = r * SIDE + lax.rem(x + w, SIDE)
            send(
                hbuf.at[now, band_of(d), :],
                recvh.at[now, :, pl.ds(pl.multiple_of(me * rows, rows), rows)],
                h_send,
                h_recv.at[c],
                d,
            )

    arrange(0)
    each("a1", (0,), go)
    each("b1", (0,), go)

    pltpu.make_async_copy(
        all_slots.at[pl.ds(0, pairs - 1)], all_slots.at[pl.ds(0, pairs - 1)], slot_recv
    ).wait()
    lists = fetch(0, all_slots, slot_lists)
    share_landed((SIDE - 1) * SIDE * two_here, 0, 2)
    share_landed((SIDE - 1) * SIDE * two_here, 1, 3)
    for k in range(tiles // 2):
        full[tiles // 2 + k] = swapped(full[k])
    lists.wait()

    def hand_out(first, last):
        @pl.loop(first, last)
        def _(k):
            p = lax.rem(pair + pairs // 2 + k, pairs)

            for u in range(in_domain // 2):
                ready[p, :, u * 2 * TILE : (u + 1) * 2 * TILE] = jnp.where(
                    low[: full.shape[1]],
                    full[slot_lists[p, 0, 2 * u]],
                    full[slot_lists[p, 0, 2 * u + 1]],
                )

            for b in range(per):
                src = ready.at[p, b * SHARE : (b + 1) * SHARE, :]
                start = pl.multiple_of((pair * per + b) * blk + keep, SHARE)
                dst = dt.at[pl.ds(start, SHARE), :]

                @pl.when(p != pair)
                def _():
                    pltpu.make_async_remote_copy(
                        src, dst, share_out, share_in, device_id=(p, me), device_id_type=MESH
                    ).start()

                @pl.when(p == pair)
                def _():
                    pltpu.make_async_copy(src, dst, share_in).start()

    hand_out(0, 3)
    for h in (0, 1):
        for sign in (1, -1):
            message("a1", h, 0, sign).wait_recv()
            message("a2", h, 0, sign).start()
    each("b1", (1, -1), go)
    hand_out(3, 5)
    each("b1", (0,), landed)
    each("b2", (0,), go)
    each("a2", (0,), landed)
    each("b1", (2,), go)
    hand_out(5, pairs)
    each("b2", (0,), landed)
    each("b1", (1, -1), landed)
    each("b2", (1, -1), go)
    each("b1", (2,), landed)
    each("b2", (2,), go)

    each("b2", (1, -1, 2), landed)
    all_shares = dt.at[pl.ds(0, PLANE * SHARE), :]
    pltpu.make_async_copy(all_shares, all_shares, share_in).wait()
    get_amp.wait()

    @pl.loop(0, chunks)
    def _(c):
        @pl.loop(0, SIDE)
        def _(k):
            half(c, lax.rem(y + k + 1, SIDE))

    def project(c):
        now = pl.ds(c * CHUNK, CHUNK)
        pltpu.make_async_copy(recvh.at[now], recvh.at[now], h_recv.at[c]).wait()
        left = recvh[now].reshape(CHUNK * blk, width)
        step = 256
        for n in range(rank // step):
            cols = slice(n * step, (n + 1) * step)
            part = dot(left, dt[cols, :], NT).astype(bf16)
            proj[now, :, cols] = part.reshape(CHUNK, blk, step)
        pltpu.make_async_remote_copy(
            proj.at[now], below.at[now], p_send.at[0], below_sem.at[c],
            device_id=(after, me), device_id_type=MESH,
        ).start()
        pltpu.make_async_remote_copy(
            proj.at[now], above.at[now], p_send.at[1], above_sem.at[c],
            device_id=(before, me), device_id_type=MESH,
        ).start()

    def finish(c):
        now = pl.ds(c * CHUNK, CHUNK)
        pltpu.make_async_copy(below.at[now], below.at[now], below_sem.at[c]).wait()
        pltpu.make_async_copy(above.at[now], above.at[now], above_sem.at[c]).wait()
        for i in range(CHUNK):
            mid = proj[c * CHUNK + i].astype(f32)
            hole = (
                columns[0][:, :1] * below[c * CHUNK + i].astype(f32)
                + columns[1][:, :1] * mid
                + columns[2][:, :1] * above[c * CHUNK + i].astype(f32)
            )
            dressed[i * blk : (i + 1) * blk, :] = (
                coupling[...].astype(f32) * mid + hole
            ).astype(bf16)

        @pl.loop(0, SIDE)
        def _(k):
            r = lax.rem(y + k + 1, SIDE)
            cols = pl.ds(pl.multiple_of(r * SIDE * rows, SIDE * rows), SIDE * rows)
            part = dot(dressed[...], dt[:, cols], NN).astype(bf16)
            bbuf[now, :, cols] = part.reshape(CHUNK, blk, SIDE * rows)
            for w in range(SIDE):
                d = r * SIDE + lax.rem(x + w, SIDE)
                src = bbuf.at[now, :, pl.ds(pl.multiple_of(d * rows, rows), rows)]
                send(src, recvb.at[now, own, :], b_send, b_recv.at[c], d)

    @pl.loop(0, chunks + 1)
    def _(c):
        @pl.when(c < chunks)
        def _():
            project(c)

        @pl.when(c > 0)
        def _():
            finish(c - 1)

    @pl.loop(0, chunks)
    def _(c):
        now = pl.ds(c * CHUNK, CHUNK)
        pltpu.make_async_copy(recvb.at[now], recvb.at[now], b_recv.at[c]).wait()

        @pl.when(c < chunks - 1)
        def _():
            left = ladder_left(recvb, c)
            for cols in ladder_steps(width):
                ladder_part(left, c, cols, dt, amp, col, row, occ_i, ladder, c)

    def sent(ref, sem):
        pltpu.make_async_copy(ref, ref, sem).wait()

    sent(pack.at[:, pl.ds(0, (PLANE - 1) * keep), :], pack_sem)
    sent(all_slots.at[pl.ds(0, pairs - 1)], slot_send)
    units = (SIDE - 1) * (2 + 2 * SIDE) * two_here
    sent(full.at[pl.ds(0, units // 2)], full_send)
    sent(ready.at[pl.ds(0, pairs - 1)], share_out)
    sent(hbuf.at[:, pl.ds(blk, (PLANE - 1) * blk), :], h_send)
    sent(proj, p_send.at[0])
    sent(proj, p_send.at[1])
    sent(bbuf.at[:, :, pl.ds(rows, (PLANE - 1) * rows)], b_send)
    for kind, offsets in (("a1", (0,)), ("a2", (0,)), ("b1", (0, 1, -1, 2)), ("b2", (0, 1, -1, 2))):
        each(kind, offsets, lambda m: m.wait_send())


def on_device(amplitudes, factor, home, domains, coupling, hole_weight, virt_energy, occ_i, occ_j):
    pairs = lax.axis_size("pair")
    ni, rows, width = amplitudes.shape[1:]
    stored, rank = factor.shape
    tiles_here = stored // TILE
    tiles = home.shape[0]
    blk = rank // PLANE
    lines = virt_energy.shape[0] // (2 * TILE)

    f32, bf16, i32 = jnp.float32, jnp.bfloat16, jnp.int32
    dma = pltpu.SemaphoreType.DMA
    chunks = ni // CHUNK
    done = ni - CHUNK
    vmem = pl.BlockSpec(memory_space=pltpu.VMEM)
    smem = pl.BlockSpec(memory_space=pltpu.SMEM)
    hbm = pl.BlockSpec(memory_space=pltpu.HBM)
    held = pl.pallas_call(
        residual_kernel,
        out_shape=(
            pltpu.VMEM((done, rows, width), f32),
            pltpu.VMEM((ni * rows, width), bf16),
            pltpu.VMEM((rank, width), bf16),
            pltpu.VMEM((ni, rank, rows), bf16),
            pltpu.VMEM((1, width), f32),
            pltpu.VMEM((rows, rows), f32),
        ),
        in_specs=[hbm] * 8 + [smem],
        out_specs=(vmem,) * 6,
        scratch_shapes=[
            pltpu.VMEM((tiles_here, TILE, rank), bf16),
            pltpu.VMEM((1, tiles), i32),
            pltpu.VMEM(domains.shape, i32),
            pltpu.VMEM((blk, rank), bf16),
            pltpu.VMEM((3, blk), bf16),
            pltpu.VMEM((lines, 2 * TILE), f32),
            pltpu.SMEM((ni,), f32),
            pltpu.VMEM((8, 128), i32),
            pltpu.SMEM((8, 128), i32),
            pltpu.VMEM((3, blk, 128), f32),
            pltpu.VMEM((pairs, 1, 128), i32),
            pltpu.SMEM((pairs, 1, 128), i32),
            pltpu.VMEM((tiles, PLANE * SHARE // pairs, 2 * TILE), bf16),
            pltpu.VMEM((pairs, PLANE * SHARE // pairs, width), bf16),
            pltpu.VMEM((CAP // 2, rank, 2 * TILE), bf16),
            pltpu.VMEM((PLANE * CAP // 2, blk - SHARE, 2 * TILE), bf16),
            pltpu.VMEM((ni, rank, rows), bf16),
            pltpu.VMEM((ni, blk, width), bf16),
            pltpu.VMEM((ni, blk, rank), bf16),
            pltpu.VMEM((ni, blk, rank), bf16),
            pltpu.VMEM((ni, blk, rank), bf16),
            pltpu.VMEM((CHUNK * blk, rank), bf16),
            pltpu.VMEM((ni, blk, width), bf16),
            dma((8,)),
            dma,
            dma,
            dma,
            dma((4,)),
            dma,
            dma,
            dma,
            dma((2,)),
            dma((40,)),
            dma((40,)),
            dma,
            dma((chunks,)),
            dma((2,)),
            dma((chunks,)),
            dma((chunks,)),
            dma,
            dma((chunks,)),
        ],
        compiler_params=pltpu.CompilerParams(
            collective_id=0, has_side_effects=True, vmem_limit_bytes=40 * 2**20
        ),
    )(
        factor.reshape(tiles_here, TILE, rank),
        home[None, :],
        domains,
        amplitudes.reshape(ni * rows, width),
        coupling,
        hole_weight[0],
        virt_energy.reshape(lines, 2 * TILE),
        occ_i,
        occ_j,
    )
    residual = pl.pallas_call(
        last_kernel,
        out_shape=jax.ShapeDtypeStruct((ni, rows, width), f32),
        in_specs=[smem] + [vmem] * 6,
        out_specs=hbm,
        scratch_shapes=[
            pltpu.VMEM((CHUNK, rows, width), f32),
            dma((done,)),
            dma((len(ladder_steps(width)),)),
        ],
        compiler_params=pltpu.CompilerParams(vmem_limit_bytes=16 * 2**20),
    )(occ_i, *held)
    return residual[None]


def solution(mesh):
    placed = (
        P("pair", None, "virt", None),
        P("virt", None),
        P(),
        P("pair", None),
        P("virt", None),
        P("pair", None, "virt"),
        P(),
        P(),
        P("pair"),
    )
    return jax.shard_map(
        on_device,
        mesh=mesh,
        in_specs=placed,
        out_specs=P("pair", None, "virt", None),
        check_vma=False,
    )
```
